32 devices in a mesh: batch: 8 (over y, x, core), seq: 4 (over z).
Axes of the slice: x: 2, y: 2, z: 4, core: 2. Of those that a mesh axis runs over, the one named last changes fastest.
Arguments:
- hidden_in: bfloat16 [32, 512, 768], P('batch', 'seq'), may hold values from -6 to 6
- segment_ids: int32 [32, 512], P('batch'), may hold values from 0 to 3, as said below
- pad_mask: int32 [32, 512], P('batch'), may hold values from 0 to 1, as said below
- cotangent: bfloat16 [32, 512, 768], P('batch', 'seq'), may hold values from -6 to 6
- w_query: bfloat16 [768, 768], P(('batch', 'seq')), may hold values from -0.21875 to 0.21875
- bias_query: bfloat16 [768], P(('batch', 'seq')), may hold values from -3 to 3
- w_key: bfloat16 [768, 768], P(('batch', 'seq')), may hold values from -0.21875 to 0.21875
- w_value: bfloat16 [768, 768], P(('batch', 'seq')), may hold values from -0.21875 to 0.21875
- bias_value: bfloat16 [768], P(('batch', 'seq')), may hold values from -3 to 3
- w_out: bfloat16 [768, 768], P(('batch', 'seq')), may hold values from -1.75 to 1.75
- bias_out: bfloat16 [768], P(('batch', 'seq')), may hold values from -3 to 3
- gain_attn: bfloat16 [768], P(('batch', 'seq')), may hold values from 0.5 to 1.5
- shift_attn: bfloat16 [768], P(('batch', 'seq')), may hold values from -3 to 3
- w_up: bfloat16 [768, 3072], P(('batch', 'seq')), may hold values from -0.21875 to 0.21875
- bias_up: bfloat16 [3072], P(('batch', 'seq')), may hold values from -3 to 3
- w_down: bfloat16 [3072, 768], P(('batch', 'seq')), may hold values from -0.109375 to 0.109375
- bias_down: bfloat16 [768], P(('batch', 'seq')), may hold values from -3 to 3
- gain_ffn: bfloat16 [768], P(('batch', 'seq')), may hold values from 0.5 to 1.5
- shift_ffn: bfloat16 [768], P(('batch', 'seq')), may hold values from -3 to 3
Outputs:
- block_out: bfloat16 [32, 512, 768], P('batch', 'seq')
- grad_in: bfloat16 [32, 512, 768], P('batch', 'seq')
- grad_w_query: float32 [768, 768], P(('batch', 'seq'))
- grad_bias_query: float32 [768], P(('batch', 'seq'))
- grad_w_key: float32 [768, 768], P(('batch', 'seq'))
- grad_w_value: float32 [768, 768], P(('batch', 'seq'))
- grad_bias_value: float32 [768], P(('batch', 'seq'))
- grad_w_out: float32 [768, 768], P(('batch', 'seq'))
- grad_bias_out: float32 [768], P(('batch', 'seq'))
- grad_gain_attn: float32 [768], P(('batch', 'seq'))
- grad_shift_attn: float32 [768], P(('batch', 'seq'))
- grad_w_up: float32 [768, 3072], P(('batch', 'seq'))
- grad_bias_up: float32 [3072], P(('batch', 'seq'))
- grad_w_down: float32 [3072, 768], P(('batch', 'seq'))
- grad_bias_down: float32 [768], P(('batch', 'seq'))
- grad_gain_ffn: float32 [768], P(('batch', 'seq'))
- grad_shift_ffn: float32 [768], P(('batch', 'seq'))
The draws below stay inside these ranges and needn't reach their ends.
Inputs may be any that keep to these rules, and one draw needn't show every extreme that they name: `segment_ids`: along each row the document numbers never fall and start at 0; a row holds at most four documents; every document begins with a real token; in the rows of each index of batch at least one row is a single document and another holds exactly four. `pad_mask`: Padding, where a row has any, is a tail of the row that lies inside the row's last document, at most 128 positions long.
All inputs are finite; a program needn't handle non-finite values.
Results may differ from the reference program's by a relative error of at most 0.015.
Values may be sent and summed in bfloat16 or wider, within the bound.
A program may use at most 256 MiB of HBM per device.

```python
import math
import jax
import jax.numpy as jnp
from jax import lax

D = 768
HEADS = 12
HEAD_DIM = 64
FF = 3072
SEQS_DEV = 1
MICRO = 4
LENGTH = 512
ROWS = 32


def layout(key):
    base_key = jax.random.fold_in(key, 11)
    cut_key, pad_key, whole_key = jax.random.split(base_key, 3)
    rows_block = SEQS_DEV * MICRO
    positions = jnp.arange(LENGTH, dtype=jnp.int32)
    cut_flags = (jax.random.randint(cut_key, (ROWS, LENGTH), 0, max(LENGTH // 8, 2)) == 0).astype(jnp.int32)
    inside = ((positions >= 1) & (positions < 3 * LENGTH // 4)).astype(jnp.int32)
    pad_len = jax.random.randint(pad_key, (ROWS, 1), 0, LENGTH // 4 + 1).astype(jnp.int32)
    chosen = jax.random.randint(whole_key, (ROWS // rows_block,), 0, rows_block).astype(jnp.int32)
    row_place = jnp.arange(ROWS, dtype=jnp.int32) % rows_block
    chosen_rows = jnp.repeat(chosen, rows_block)
    single = (row_place == chosen_rows).astype(jnp.int32)[:, None]
    busy = (row_place == (chosen_rows + 1) % rows_block).astype(jnp.int32)[:, None]
    forced = ((positions == LENGTH // 8) | (positions == LENGTH // 4) | (positions == 3 * LENGTH // 8)).astype(jnp.int32)
    cut_flags = jnp.maximum(cut_flags, busy * forced[None, :])
    cut_flags = cut_flags * inside[None, :] * (1 - single)
    pad_len = pad_len * (1 - single)
    segments = jnp.minimum(jnp.cumsum(cut_flags, axis=1), 3).astype(jnp.int32)
    live_flags = (positions[None, :] < LENGTH - pad_len).astype(jnp.int32)
    return (segments, live_flags)


def draw_segment_ids(key, part):
    segments, live_flags = layout(key)
    return segments


def draw_pad_mask(key, part):
    segments, live_flags = layout(key)
    return live_flags


def levels(stream_key, shape, cuts, least, top_value):
    factor_of = 1.0
    for position, parts in cuts:
        draws = jax.random.uniform(jax.random.fold_in(jax.random.fold_in(stream_key, 6), position), (parts,), jnp.float32, least / len(cuts), top_value / len(cuts))
        factor_of = factor_of * jnp.repeat(jnp.exp(draws), shape[position] // parts).reshape((-1,) + (1,) * (len(shape) - 1 - position))
    return factor_of


def centred(rng, extent, width, bound, cuts=(), kind=jnp.bfloat16):
    values = jax.random.normal(rng, extent, jnp.float32) * width
    if len(cuts) > 0:
        values = levels(rng, extent, cuts, -0.22, 0.18) * values
    return jnp.clip(values, min=-bound, max=bound).astype(kind)


def setup_inputs(seed: int = 0) -> dict:
    keys = jax.random.split(jax.random.key(seed), 20)
    return {
        "hidden_in": centred(keys[0], (ROWS, LENGTH, D), 1.0, 6.0, ((0, 8), (1, 4))),
        "segment_ids": draw_segment_ids(jax.random.fold_in(keys[19], 71), 0),
        "pad_mask": draw_pad_mask(jax.random.fold_in(keys[19], 71), 0),
        "cotangent": centred(keys[3], (ROWS, LENGTH, D), 1.0, 6.0, ((0, 8), (1, 4))),
        "w_query": centred(keys[4], (D, D), D ** -0.5, 0.21875, ((0, 32),)),
        "bias_query": centred(keys[5], (D,), 0.5, 3.0, ((0, 32),)),
        "w_key": centred(keys[6], (D, D), D ** -0.5, 0.21875, ((0, 32),)),
        "w_value": centred(keys[7], (D, D), D ** -0.5, 0.21875, ((0, 32),)),
        "bias_value": centred(keys[8], (D,), 0.5, 3.0, ((0, 32),)),
        "w_out": centred(keys[9], (D, D), (D * 8 // LENGTH) ** -0.5, 1.75, ((0, 32),)),
        "bias_out": centred(keys[10], (D,), 0.5, 3.0, ((0, 32),)),
        "gain_attn": jnp.clip(1.0 + 0.1 * jax.random.normal(keys[11], (D,), jnp.float32), 0.5, 1.5).astype(jnp.bfloat16),
        "shift_attn": centred(keys[12], (D,), 0.5, 3.0, ((0, 32),)),
        "w_up": centred(keys[13], (D, FF), D ** -0.5, 0.21875, ((0, 32),)),
        "bias_up": centred(keys[14], (FF,), 0.5, 3.0, ((0, 32),)),
        "w_down": centred(keys[15], (FF, D), FF ** -0.5, 0.109375, ((0, 32),)),
        "bias_down": centred(keys[16], (D,), 0.5, 3.0, ((0, 32),)),
        "gain_ffn": jnp.clip(1.0 + 0.1 * jax.random.normal(keys[17], (D,), jnp.float32), 0.5, 1.5).astype(jnp.bfloat16),
        "shift_ffn": centred(keys[18], (D,), 0.5, 3.0, ((0, 32),)),
    }


@jax.custom_vjp
def low(v):
    return lax.optimization_barrier(v.astype(jnp.bfloat16)).astype(jnp.float32)

@jax.custom_vjp
def low_back(v):
    return v

def low_keep(v):
    return (low(v), None)

def low_pass(kept, grad):
    return (grad,)

def back_keep(v):
    return (v, None)

def back_low(kept, grad):
    return (low(grad),)
low.defvjp(low_keep, low_pass)
low_back.defvjp(back_keep, back_low)
norm_eps = 1e-05
masked_score = -1000000000.0

def layer_norm(values, norm_gain, norm_shift):
    center = values - lax.optimization_barrier(jnp.mean(values, axis=-1, keepdims=True))
    spread = lax.optimization_barrier(jnp.mean(center * center, axis=-1, keepdims=True))
    return center * lax.rsqrt(spread + norm_eps) * norm_gain + norm_shift

def matmul(left_side, right_side):
    return jnp.einsum('gtd,de->gte', left_side, right_side, precision=lax.Precision.HIGHEST)

def forward(params, hidden, allowed):
    w_query, bias_query, w_key, w_value, bias_value, w_out, bias_out, gain_attn, shift_attn, w_up, bias_up, w_down, bias_down, gain_ffn, shift_ffn = params
    groups, seq_length, model_width = hidden.shape
    heads_shape = (groups, seq_length, HEADS, HEAD_DIM)
    queries = low_back(low(matmul(hidden, w_query) + bias_query)).reshape(heads_shape)
    key_heads = low_back(low(matmul(hidden, w_key))).reshape(heads_shape)
    value_heads = low_back(low(matmul(hidden, w_value) + bias_value)).reshape(heads_shape)
    scores = low_back(jnp.einsum('gqhd,gkhd->ghqk', queries, key_heads, precision=lax.Precision.HIGHEST) * 0.125)
    scores = jnp.where(allowed[:, None], scores, masked_score)
    shifted = scores - lax.optimization_barrier(jnp.max(scores, axis=-1, keepdims=True))
    exp_scores = jnp.exp(shifted)
    probability = low(exp_scores / lax.optimization_barrier(jnp.sum(exp_scores, axis=-1, keepdims=True)))
    attended = jnp.einsum('ghqk,gkhd->gqhd', probability, value_heads, precision=lax.Precision.HIGHEST)
    attended = low_back(low(attended.reshape(groups, seq_length, model_width)))
    attn_out = low_back(matmul(attended, w_out) + bias_out)
    normed = layer_norm(hidden + attn_out, gain_attn, shift_attn)
    inner_sum = low_back(matmul(low(normed), w_up) + bias_up)
    activated = low(jax.nn.gelu(inner_sum, approximate=True))
    ffn_out = low_back(matmul(activated, w_down) + bias_down)
    return layer_norm(normed + ffn_out, gain_ffn, shift_ffn)

def reference(hidden_in, segment_ids, pad_mask, cotangent, w_query, bias_query, w_key, w_value, bias_value, w_out, bias_out, gain_attn, shift_attn, w_up, bias_up, w_down, bias_down, gain_ffn, shift_ffn):
    params = tuple((member.astype(jnp.float32) for member in (w_query, bias_query, w_key, w_value, bias_value, w_out, bias_out, gain_attn, shift_attn, w_up, bias_up, w_down, bias_down, gain_ffn, shift_ffn)))
    group_rows = math.gcd(ROWS, max(1, 4096 // LENGTH))
    steps_count = ROWS // group_rows

    def split_rows(whole_array):
        return whole_array.reshape((steps_count, group_rows) + whole_array.shape[1:])

    def accumulate(totals, scan_item):
        hidden_group, segment_group, live_group, cot_group = scan_item
        allowed = (segment_group[:, :, None] == segment_group[:, None, :]) & (live_group[:, None, :] == 1)

        def apply_layer(hidden_float, params_float):
            return forward(params_float, hidden_float, allowed)
        result, pullback = jax.vjp(apply_layer, hidden_group.astype(jnp.float32), params)
        grad_hidden, grad_params = pullback(cot_group.astype(jnp.float32))
        totals = jax.tree.map(lambda total_one, total_two: total_one + total_two, totals, grad_params)
        return (totals, (result.astype(jnp.bfloat16), grad_hidden.astype(jnp.bfloat16)))
    initial = tuple((jnp.zeros_like(member) for member in params))
    totals, (outputs, input_grads) = lax.scan(accumulate, initial, (split_rows(hidden_in), split_rows(segment_ids), split_rows(pad_mask), split_rows(cotangent)))
    return (outputs.reshape(ROWS, LENGTH, D), input_grads.reshape(ROWS, LENGTH, D), totals[0], totals[1], totals[2], totals[3], totals[4], totals[5], totals[6], totals[7], totals[8], totals[9], totals[10], totals[11], totals[12], totals[13], totals[14])
```

```python
import jax
import jax.numpy as jnp
from jax import lax
from jax.experimental import pallas as pl
from jax.experimental.pallas import tpu as pltpu
from jax.sharding import PartitionSpec as P

BF = jnp.bfloat16
F32 = jnp.float32
MESH = pl.DeviceIdType.MESH
EPS = 1e-5
NEG = -1e9
C0 = 0.7978845608028654
C1 = 0.044715
NN = (((1,), (0,)), ((), ()))
NT = (((1,), (1,)), ((), ()))
TN = (((0,), (0,)), ((), ()))
VMEM = pltpu.VMEM
ANY = pl.ANY
ROW_BQ, ROW_BV, ROW_BO, ROW_GA, ROW_SA, ROW_BD, ROW_GF, ROW_SF, ROW_UP = 0, 2, 3, 4, 5, 6, 7, 8, 9
VROWS = 16


def dg(a, b, dims):
    return lax.dot_general(a, b, dims, preferred_element_type=F32)


def ds(start, size):
    return pl.ds(pl.multiple_of(start, size), size)


class Place:
    def __init__(self, fold):
        bidx = lax.axis_index("batch")
        z = lax.axis_index("seq")
        hi = bidx // fold
        lo = bidx % fold
        y = hi // 4
        x = (hi // 2) % 2
        c = hi % 2
        self.y, self.x, self.c, self.z, self.b = y, x, c, z, hi
        self.k = hi * 4 + z
        self.bx = y * 4 + (1 - x) * 2 + c
        self.by = (1 - y) * 4 + x * 2 + c
        self.bd = (1 - y) * 4 + (1 - x) * 2 + c
        self.bc = y * 4 + x * 2 + (1 - c)

        def dev(block):
            return (block * fold + lo, z)

        self.xdev, self.ydev, self.cdev = dev(self.bx), dev(self.by), dev(self.bc)
        self.zidx = [lax.rem(z + k, 4) for k in (1, 2, 3)]
        self.zfrom = [lax.rem(z + 4 - k, 4) for k in (1, 2, 3)]
        self.zdev = [(bidx, zi) for zi in self.zidx]

    def greet(self):
        bar = pltpu.get_barrier_semaphore()
        for d in [self.xdev, self.ydev, self.cdev] + self.zdev:
            pl.semaphore_signal(bar, inc=1, device_id=d, device_id_type=MESH)
        pl.semaphore_wait(bar, 6)


class Wire:
    def __init__(self, send_sems, recv_sems):
        self.ss, self.rs, self.n, self.open = send_sems, recv_sems, 0, []

    def send(self, src, dst, device):
        i = self.n
        self.n += 1
        cp = pltpu.make_async_remote_copy(src_ref=src, dst_ref=dst, send_sem=self.ss.at[i], recv_sem=self.rs.at[i],
                                          device_id=device, device_id_type=MESH)
        cp.start()
        self.open.append(cp)
        return (i, device, cp)

    def recv(self, tag, dst):
        i, device, _ = tag
        pltpu.make_async_remote_copy(src_ref=dst, dst_ref=dst, send_sem=self.ss.at[i], recv_sem=self.rs.at[i],
                                     device_id=device, device_id_type=MESH).wait_recv()

    def sent(self, tag):
        tag[2].wait_send()
        self.open = [cp for cp in self.open if cp is not tag[2]]

    def finish(self):
        for cp in self.open:
            cp.wait_send()
        self.open = []


class Local:
    def __init__(self, sems):
        self.sems, self.n, self.open = sems, 0, []

    def start(self, src, dst):
        cp = pltpu.make_async_copy(src, dst, self.sems.at[self.n])
        self.n += 1
        cp.start()
        self.open.append(cp)
        return cp

    def wait(self, cp):
        cp.wait()
        self.open = [other for other in self.open if other is not cp]

    def finish(self):
        for cp in self.open:
            cp.wait()
        self.open = []


def norm_rows(v, gain, shift):
    center = v - jnp.mean(v, axis=-1, keepdims=True)
    inv = lax.rsqrt(jnp.mean(center * center, axis=-1, keepdims=True) + EPS)
    xhat = center * inv
    return xhat * gain + shift, xhat, inv


def norm_back(g, xhat, inv, gain):
    e = g * gain
    return inv * (e - jnp.mean(e, axis=-1, keepdims=True) - xhat * jnp.mean(e * xhat, axis=-1, keepdims=True))


def rows_sum(v):
    return jnp.sum(v, axis=0, keepdims=True)


def place_matrix(rows, width, start, count):
    i = lax.broadcasted_iota(jnp.int32, (rows, width), 0)
    j = lax.broadcasted_iota(jnp.int32, (rows, width), 1)
    return jnp.where((j == start + i) & (i < count), 1.0, 0.0).astype(BF)


def segments(seg_ref, pad_ref, z, length):
    seg = seg_ref[pl.ds(z, 1), :].astype(F32)
    live = pad_ref[pl.ds(z, 1), :]
    keyed = jnp.where(live == 1, seg, -1.0)

    def column(row):
        return jnp.broadcast_to(row, (128, length)).T[:, 0:1]

    return seg, keyed, column


def forward_kernel(fold, T, D, FF, r, rd,
                   hidden, cot, seg, pad, wq, wk, wv, wo, wu, wd, vin,
                   o_tok, o_qkv, o_att, o_lse, o_nlow, o_xh1, o_inv1, o_act, o_gp, o_gmid, o_gffn, o_out, o_vec,
                   o_gvec, o_wA, o_wU, o_wD,
                   zA, zU, wA, wU, wD, tok, cotr, qkv, att, lse, nlow, xh1, inv1, normed, act, gp, tmp, gffn, out,
                   vec, gvec, vsend, vland, ss, rs, ls):
    me = Place(fold)
    wire = Wire(ss, rs)
    local = Local(ls)
    z, b = me.z, me.b
    Q = T // 4
    own = []
    for i, w in enumerate((wq, wk, wv, wo)):
        own.append(local.start(w, zA.at[i, z]))
    own_u = local.start(wu, zU.at[z])
    own_d = local.start(wd, wD.at[b // 2, ds((b % 2) * (4 * rd) + z * rd, rd)])
    own_t = local.start(hidden.at[z], tok.at[ds(z * Q, Q)])
    own_c = local.start(cot.at[z], cotr.at[ds(z * Q, Q)])

    v_a = dg(vin[...], place_matrix(128, D, me.k * r, r), NN)
    up_width = 32 * 4 * r // (FF // D)
    per_row = D // (4 * r)
    v_u = dg(vin[...], place_matrix(128, D, (me.k % per_row) * (4 * r), 4 * r), NN)[ROW_UP:ROW_UP + 1]
    ri = lax.broadcasted_iota(jnp.int32, (VROWS, D), 0)
    vsend[0] = jnp.where(ri < ROW_UP, v_a, jnp.where(ri == ROW_UP + me.k // per_row, jnp.broadcast_to(v_u, (VROWS, D)), 0.0)).astype(BF)

    me.greet()

    def zsend(pairs):
        return [[wire.send(s, d, me.zdev[k]) for (s, d) in pairs(k)] for k in range(3)]

    def zrecv(tags, dsts):
        for k in range(3):
            for tag, dst in zip(tags[k], dsts(k)):
                wire.recv(tag, dst)

    t_vec = zsend(lambda k: [(vsend.at[0], vland.at[k])])
    t_qkv = zsend(lambda k: [(w, zA.at[i, z]) for i, w in enumerate((wq, wk, wv))])
    t_u = zsend(lambda k: [(wu, zU.at[z])])
    t_o = zsend(lambda k: [(wo, zA.at[3, z])])
    t_hid = zsend(lambda k: [(hidden.at[me.zidx[k]], tok.at[ds(z * Q, Q)])])

    def drow(block, sub):
        return wD.at[block // 2, ds((block % 2) * (4 * rd) + sub * rd, rd)]

    t_d = zsend(lambda k: [(wd, drow(b, z))])
    t_cot = zsend(lambda k: [(cot.at[me.zidx[k]], cotr.at[ds(z * Q, Q)])])

    class Spread:
        def __init__(self, region):
            self.region = region

        def own(self):
            g = self.region
            self.tx = wire.send(g(b, 0, 2), g(b, 0, 2), me.xdev)
            self.ty = wire.send(g(b, 0, 2), g(b, 0, 2), me.ydev)
            self.tc = [wire.send(g(b, 0, 2), g(b, 0, 2), me.cdev)]

        def mid(self):
            g = self.region
            wire.recv(self.tx, g(me.bx, 0, 2))
            self.f1 = wire.send(g(me.bx, 0, 1), g(me.bx, 0, 1), me.ydev)
            wire.recv(self.ty, g(me.by, 0, 2))
            self.f2 = wire.send(g(me.by, 1, 1), g(me.by, 1, 1), me.xdev)
            self.tc.append(wire.send(g(me.bx, 0, 2), g(me.bx, 0, 2), me.cdev))
            self.tc.append(wire.send(g(me.by, 0, 2), g(me.by, 0, 2), me.cdev))

        def last(self):
            g = self.region
            wire.recv(self.f1, g(me.bd, 0, 1))
            wire.recv(self.f2, g(me.bd, 1, 1))
            self.tc.append(wire.send(g(me.bd, 0, 2), g(me.bd, 0, 2), me.cdev))

        def done(self):
            g = self.region
            for tag, block in zip(self.tc, (me.b, me.bx, me.by, me.bd)):
                other = block + 1 - 2 * me.c
                wire.recv(tag, g(other, 0, 2))

    h = 2 * r
    s_qkv = Spread(lambda k, half, n: wA.at[0:3, ds(k * 4 * r + half * h, h) if n == 1 else ds(k * 4 * r, 4 * r)])
    s_o = Spread(lambda k, half, n: wA.at[3, ds(k * 4 * r + half * h, h) if n == 1 else ds(k * 4 * r, 4 * r)])
    s_u = Spread(lambda k, half, n: wU.at[ds(k * 4 * r + half * h, h) if n == 1 else ds(k * 4 * r, 4 * r)])
    hd = 2 * rd
    s_d = Spread(lambda k, half, n: wD.at[k // 2, ds((k % 2) * 4 * rd + half * hd, hd) if n == 1 else ds((k % 2) * 4 * rd, 4 * rd)])

    def join(parts):
        return jnp.concatenate([p.astype(F32) for p in parts], axis=0).astype(BF)

    zrecv(t_vec, lambda k: [vland.at[k]])
    vsend[1] = vsend[0] + vland[0] + vland[1] + vland[2]
    tv = wire.send(vsend.at[1], vland.at[3], me.xdev)

    for cp in own:
        local.wait(cp)
    zrecv(t_qkv, lambda k: [zA.at[i, me.zfrom[k]] for i in range(3)])
    for i in range(3):
        wA[i, ds(b * 4 * r, 4 * r), :] = join([zA[i, s] for s in range(4)])
    s_qkv.own()
    wire.recv(tv, vland.at[3])
    vsend[2] = vsend[1] + vland[3]
    tv = wire.send(vsend.at[2], vland.at[4], me.ydev)

    local.wait(own_u)
    zrecv(t_u, lambda k: [zU.at[me.zfrom[k]]])
    wU[ds(b * 4 * r, 4 * r), :] = join([zU[s] for s in range(4)])
    s_u.own()
    wire.recv(tv, vland.at[4])
    vsend[3] = vsend[2] + vland[4]
    tv = wire.send(vsend.at[3], vland.at[5], me.cdev)
    s_qkv.mid()
    zrecv(t_o, lambda k: [zA.at[3, me.zfrom[k]]])
    wA[3, ds(b * 4 * r, 4 * r), :] = join([zA[3, s] for s in range(4)])
    s_o.own()
    s_qkv.last()
    wire.recv(tv, vland.at[5])
    vec[...] = vsend[3].astype(F32) + vland[5].astype(F32)
    local.start(vec, o_vec)
    s_qkv.done()
    local.wait(own_t)
    zrecv(t_hid, lambda k: [tok.at[ds(me.zfrom[k] * Q, Q)]])
    local.start(tok, o_tok)
    s_u.mid()

    def project(j):
        v = dg(tok[...], wA[j], NN) + vec[pl.ds(j, 1), :]
        v = v.astype(BF)
        qkv[j] = v * jnp.where(j == 0, 0.125, 1.0).astype(BF)

    pl.loop(0, 3)(project)
    local.start(qkv, o_qkv)
    s_u.last()

    seg_row, key_row, column = segments(seg, pad, z, T)
    seg_col = column(seg_row)
    lane = lax.broadcasted_iota(jnp.int32, (T, 128), 1)
    lo = lane < 64

    def attend(p):
        o = ds(p * 128, 128)
        k = qkv[1, :, o]
        v = qkv[2, :, o]
        one = jnp.ones_like(v)
        zero = jnp.zeros_like(v)
        v0, v1 = jnp.where(lo, v, one), jnp.where(lo, one, v)
        k0, k1 = jnp.where(lo, k, zero), jnp.where(lo, zero, k)
        for step in range(T // 128):
            rows = slice(step * 128, (step + 1) * 128)
            q = qkv[0, rows, o]
            ok = seg_col[rows] == key_row
            res, top = [], []
            for kk, vv in ((k0, v0), (k1, v1)):
                s = jnp.where(ok, dg(q, kk, NT), NEG)
                m = jnp.max(s, axis=-1, keepdims=True)
                res.append(dg(jnp.exp(s - m).astype(BF), vv, NN))
                top.append(m)
            low = lo[:128]
            num = jnp.where(low, res[0], res[1])
            den = pltpu.roll(jnp.where(low, res[1], res[0]), 64, 1)
            att[rows, o] = (num / den).astype(BF)
            lt = (jnp.log(den) + jnp.where(low, top[0], top[1])).T
            lse[p, 0:1, rows] = lt[0:1]
            lse[p, 1:2, rows] = lt[64:65]

    pl.loop(0, 2)(attend)
    s_o.mid()
    local.wait(own_d)
    zrecv(t_d, lambda k: [drow(b, me.zfrom[k])])
    s_d.own()
    pl.loop(2, 4)(attend)
    s_o.last()
    pl.loop(4, 6)(attend)
    local.start(att, o_att)
    local.start(lse, o_lse)
    s_o.done()
    local.start(wA, o_wA)
    s_d.mid()

    tmp[...] = dg(att[...], wA[3], NN) + vec[ROW_BO:ROW_BO + 1, :]

    def norm_one(i):
        rr = ds(i * 64, 64)
        y_, xh, inv = norm_rows(tmp[rr, :] + tok[rr, :].astype(F32), vec[ROW_GA:ROW_GA + 1, :], vec[ROW_SA:ROW_SA + 1, :])
        normed[rr, :] = y_
        nlow[rr, :] = y_.astype(BF)
        xh1[rr, :] = xh
        inv1[rr, :] = jnp.broadcast_to(inv, (64, 128))

    pl.loop(0, T // 64)(norm_one)
    local.start(nlow, o_nlow)
    local.start(xh1, o_xh1)
    local.start(inv1, o_inv1)
    s_u.done()
    local.start(wU, o_wU)

    wide = D // 2

    def up(j):
        o = ds(j * wide, wide)
        bias = vec[pl.ds(ROW_UP + j // 2, 1), ds((j % 2) * wide, wide)]
        v = dg(nlow[...], wU[:, o], NN) + bias
        v2 = v * v
        t = jnp.tanh(v * (C0 + C0 * C1 * v2))
        half = 0.5 * (1 + t)
        act[:, o] = (v * half).astype(BF)
        gp[:, o] = (half + 0.5 * v * (1 - t * t) * (C0 + 3 * C0 * C1 * v2)).astype(BF)

    pl.loop(0, 4)(up)
    s_d.last()
    pl.loop(4, 8)(up)
    local.start(act, o_act)
    local.start(gp, o_gp)
    s_d.done()
    local.start(wD, o_wD)

    parts = FF // D
    tmp[...] = dg(act[:, 0:D], wD[0], NN) + vec[ROW_BD:ROW_BD + 1, :]

    def down(j):
        tmp[...] += dg(act[:, ds(j * D, D)], wD[j], NN)

    pl.loop(1, parts)(down)
    local.wait(own_c)
    zrecv(t_cot, lambda k: [cotr.at[ds(me.zfrom[k] * Q, Q)]])
    zero_row = jnp.zeros((1, D), F32)
    gvec[...] = jnp.zeros_like(gvec)

    def norm_two(i, sums):
        rr = ds(i * 64, 64)
        gain = vec[ROW_GF:ROW_GF + 1, :]
        y_, xh, inv = norm_rows(tmp[rr, :] + normed[rr, :], gain, vec[ROW_SF:ROW_SF + 1, :])
        out[rr, :] = y_.astype(BF)
        g = cotr[rr, :].astype(F32)
        gm = norm_back(g, xh, inv, gain)
        gl = gm.astype(BF)
        tmp[rr, :] = gm
        gffn[rr, :] = gl
        return sums[0] + rows_sum(g * xh), sums[1] + rows_sum(g), sums[2] + rows_sum(gl.astype(F32))

    s0, s1, s2 = lax.fori_loop(0, T // 64, norm_two, (zero_row, zero_row, zero_row))
    gvec[ROW_GF:ROW_GF + 1, :] = s0
    gvec[ROW_SF:ROW_SF + 1, :] = s1
    gvec[ROW_BD:ROW_BD + 1, :] = s2
    local.start(out, o_out)
    local.start(tmp, o_gmid)
    local.start(gffn, o_gffn)
    local.start(gvec, o_gvec)
    wire.finish()
    local.finish()


def backward_kernel(fold, T, D, FF, r, rd, widths,
                    seg, pad, i_tok, i_qkv, i_att, i_lse, i_nlow, i_xh1, i_inv1, i_act, i_gp, i_gmid, i_gffn, i_out,
                    i_vec, i_gvec, i_wA, i_wU, i_wD,
                    bout, gin_out, gA_out, gU_out, gD_out, gv_out,
                    w1, wU, tok, qkv, att, lse, nlow, xh1, inv1, act, gp, gmid, gffn, vec, gvec, gattn, gatt, gqkv,
                    d0_snd, d1_snd, u_snd, o_snd, a_snd,
                    own_d0, own_d1, own_u0, own_u1, own_o, own_a0, own_a1,
                    r1_d0, r1_d1, r1_u0, r1_u1, r1_o, r1_a0, r1_a1,
                    ra_d0, ra_d1, ra_u0, ra_u1, ra_o, ra_a0, ra_a1,
                    rb_d0, rb_d1, rb_u0, rb_u1, rb_o, rb_a0, rb_a1,
                    zs_d0, zs_d1, zs_u0, zs_u1, zs_o, zs_a0, zs_a1,
                    zr_d0, zr_d1, zr_u0, zr_u1, zr_o, zr_a0, zr_a1,
                    vsend, vland, ss, rs, ls):
    me = Place(fold)
    wire = Wire(ss, rs)
    local = Local(ls)
    z, b, c, x, y = me.z, me.b, me.c, me.x, me.y
    Q = T // 4
    l_act = local.start(i_act, act)
    l_gffn = local.start(i_gffn, gffn)
    l_wD = local.start(i_wD, w1)
    l_gp = local.start(i_gp, gp)
    l_nlow = local.start(i_nlow, nlow)
    l_gvec = local.start(i_gvec, gvec)
    l_gmid = local.start(i_gmid, gmid)
    l_wU = local.start(i_wU, wU)
    l_vec = local.start(i_vec, vec)
    l_xh1 = local.start(i_xh1, xh1)
    l_inv1 = local.start(i_inv1, inv1)
    l_att = local.start(i_att, att)
    l_qkv = local.start(i_qkv, qkv)
    l_lse = local.start(i_lse, lse)
    l_tok = local.start(i_tok, tok)
    local.start(i_out.at[ds(z * Q, Q)], bout.at[z])
    me.greet()
    t_out = [wire.send(i_out.at[ds(me.zidx[k] * Q, Q)], bout.at[z], me.zdev[k]) for k in range(3)]

    def keep(v0, v1):
        first = c == 0
        return jnp.where(first, v0, v1).astype(BF), jnp.where(first, v1, v0).astype(BF)

    class Sum:
        def __init__(self, snd, mine, r1, ra, rb, zs, zr, rows, write):
            self.snd, self.mine, self.r1, self.ra, self.rb, self.zs, self.zr = snd, mine, r1, ra, rb, zs, zr
            self.rows, self.write = rows, write

        def core(self):
            self.tc = wire.send(self.snd, self.r1, me.cdev)

        def plane_one(self):
            n = 2 * self.rows
            wire.recv(self.tc, self.r1)

            @pl.loop(0, 2)
            def _(i):
                for j in range(2):
                    self.mine[i, j] = (self.mine[i, j].astype(F32) + self.r1[i, j].astype(F32)).astype(BF)

            self.tx = wire.send(self.mine.at[:, 1 - x, 0:n], self.ra.at[0], me.xdev)
            self.ty = wire.send(self.mine.at[1 - y, :, n:2 * n], self.ra.at[1], me.ydev)

        def plane_two(self):
            n = 2 * self.rows
            wire.recv(self.tx, self.ra.at[0])
            for i in range(2):
                self.mine[i, x, 0:n] = (self.mine[i, x, 0:n].astype(F32) + self.ra[0, i].astype(F32)).astype(BF)
            self.ty2 = wire.send(self.mine.at[1 - y, x, 0:n], self.rb.at[0], me.ydev)
            wire.recv(self.ty, self.ra.at[1])
            for i in range(2):
                self.mine[y, i, n:2 * n] = (self.mine[y, i, n:2 * n].astype(F32) + self.ra[1, i].astype(F32)).astype(BF)
            self.tx2 = wire.send(self.mine.at[y, 1 - x, n:2 * n], self.rb.at[1], me.xdev)

        def along(self):
            n = 2 * self.rows
            q = self.rows
            for half, tag in ((0, self.ty2), (1, self.tx2)):
                wire.recv(tag, self.rb.at[half])
                v = self.mine[y, x, half * n:(half + 1) * n].astype(F32) + self.rb[half].astype(F32)
                self.zs[2 * half] = v[0:q].astype(BF)
                self.zs[2 * half + 1] = v[q:2 * q].astype(BF)
            self.tz = [wire.send(self.zs.at[me.zidx[k]], self.zr.at[k], me.zdev[k]) for k in range(3)]

        def done(self):
            v = self.zs[z].astype(F32)
            for k in range(3):
                wire.recv(self.tz[k], self.zr.at[k])
                v = v + self.zr[k].astype(F32)
            self.write(v)

    cD = [0, widths[0], D]

    def write_d(i):
        def f(v):
            gD_out[:, cD[i]:cD[i + 1]] = v
        return f

    half_ff = FF // 2

    def write_u(i):
        def f(v):
            gU_out[:, i * half_ff:(i + 1) * half_ff] = v
        return f

    def write_o(v):
        gA_out[3] = v

    hD = D // 2

    def write_a(i):
        def f(v):
            for m in range(3):
                gA_out[m, :, i * hD:(i + 1) * hD] = v[:, m * hD:(m + 1) * hD]
        return f

    D0 = Sum(d0_snd, own_d0, r1_d0, ra_d0, rb_d0, zs_d0, zr_d0, rd, write_d(0))
    D1 = Sum(d1_snd, own_d1, r1_d1, ra_d1, rb_d1, zs_d1, zr_d1, rd, write_d(1))
    U0 = Sum(u_snd, own_u0, r1_u0, ra_u0, rb_u0, zs_u0, zr_u0, r, write_u(0))
    U1 = Sum(u_snd, own_u1, r1_u1, ra_u1, rb_u1, zs_u1, zr_u1, r, write_u(1))
    O = Sum(o_snd, own_o, r1_o, ra_o, rb_o, zs_o, zr_o, r, write_o)
    A0 = Sum(a_snd, own_a0, r1_a0, ra_a0, rb_a0, zs_a0, zr_a0, r, write_a(0))
    A1 = Sum(a_snd, own_a1, r1_a1, ra_a1, rb_a1, zs_a1, zr_a1, r, write_a(1))

    local.wait(l_act)
    local.wait(l_gffn)

    def down_grad(part, cols):
        @pl.loop(0, 4)
        def _(i):
            v = dg(act[:, ds(i * D, D)], gffn[:, cols], TN)
            mine, theirs = keep(v[0:4 * rd], v[4 * rd:8 * rd])
            part.mine[i // 2, i % 2] = mine
            part.snd[i // 2, i % 2] = theirs

    def split_rows(v):
        n = 4 * r
        return [keep(v[(2 * i) * n:(2 * i + 1) * n], v[(2 * i + 1) * n:(2 * i + 2) * n]) for i in range(4)]

    def store(part, v, cols):
        for i, (mine, theirs) in enumerate(split_rows(v)):
            part.mine[i // 2, i % 2, :, cols] = mine
            part.snd[i // 2, i % 2, :, cols] = theirs

    down_grad(D0, slice(cD[0], cD[1]))
    D0.core()
    down_grad(D1, slice(cD[1], cD[2]))
    D1.core()
    D0.plane_one()
    local.wait(l_wD)
    local.wait(l_gp)
    local.wait(l_gvec)

    def inner(j):
        o = ds(j * D, D)
        gi = (dg(gffn[...], w1[j], NT) * gp[:, o].astype(F32)).astype(BF)
        gp[:, o] = gi
        gvec[pl.ds(ROW_UP + j, 1), :] = rows_sum(gi.astype(F32))

    def up_grad(part, first):
        wide = half_ff // 3

        @pl.loop(0, 3)
        def _(j):
            o = ds(j * wide, wide)
            store(part, dg(nlow[...], gp[:, ds(first + j * wide, wide)], TN), o)

    pl.loop(0, 2)(inner)
    D1.plane_one()
    local.wait(l_nlow)
    up_grad(U0, 0)
    U0.core()
    pl.loop(2, 4)(inner)
    l_wA = local.start(i_wA, w1)
    U0.plane_one()
    D0.plane_two()
    wire.sent(U0.tc)
    up_grad(U1, half_ff)
    U1.core()
    D1.plane_two()
    local.wait(l_wU)
    local.wait(l_gmid)
    gmid[...] += dg(gp[...], wU[...], NT)
    U1.plane_one()
    D0.along()
    local.wait(l_vec)
    local.wait(l_xh1)
    local.wait(l_inv1)
    zero_row = jnp.zeros((1, D), F32)

    def norm_one(i, sums):
        rr = ds(i * 64, 64)
        g = gmid[rr, :]
        xh = xh1[rr, :]
        gm = norm_back(g, xh, inv1[rr, 0:1], vec[ROW_GA:ROW_GA + 1, :])
        gl = gm.astype(BF)
        gmid[rr, :] = gm
        gattn[rr, :] = gl
        return sums[0] + rows_sum(g * xh), sums[1] + rows_sum(g), sums[2] + rows_sum(gl.astype(F32))

    s0, s1, s2 = lax.fori_loop(0, T // 64, norm_one, (zero_row, zero_row, zero_row))
    gvec[ROW_GA:ROW_GA + 1, :] = s0
    gvec[ROW_SA:ROW_SA + 1, :] = s1
    gvec[ROW_BO:ROW_BO + 1, :] = s2
    local.wait(l_att)
    store(O, dg(att[...], gattn[...], TN), slice(0, D))
    O.core()
    U0.plane_two()
    D1.along()
    local.wait(l_wA)
    gatt[...] = dg(gattn[...], w1[3], NT).astype(BF)
    local.wait(l_qkv)
    local.wait(l_lse)
    local.wait(l_tok)

    seg_row, key_row, column = segments(seg, pad, z, T)
    key_col = column(key_row)
    lane = lax.broadcasted_iota(jnp.int32, (T, 128), 1)
    lo = lane < 64
    pick = (lax.broadcasted_iota(jnp.int32, (8, 128), 1) // 64 == lax.broadcasted_iota(jnp.int32, (8, 128), 0)).astype(BF)

    def attend(p):
        o = ds(p * 128, 128)
        q = qkv[0, :, o]
        k = qkv[1, :, o]
        g = gatt[:, o]
        prod = g.astype(F32) * att[:, o].astype(F32)
        hi = prod.astype(BF)
        rest = (prod - hi.astype(F32)).astype(BF)
        delta = dg(pick, hi, NT) + dg(pick, rest, NT)
        zero = jnp.zeros_like(q)
        qm = (jnp.where(lo, q, zero), jnp.where(lo, zero, q))
        gm = (jnp.where(lo, g, zero), jnp.where(lo, zero, g))
        km = (jnp.where(lo, k, zero), jnp.where(lo, zero, k))
        dq = jnp.zeros((T, 128), F32)
        for step in range(T // 128):
            rows = slice(step * 128, (step + 1) * 128)
            kc = qkv[1, rows, o]
            vc = qkv[2, rows, o]
            ok = key_col[rows] == seg_row
            dk = jnp.zeros((128, 128), F32)
            dv = jnp.zeros((128, 128), F32)
            for hh in range(2):
                s = jnp.where(ok, dg(kc, qm[hh], NT), NEG)
                pt = jnp.exp(s - lse[p, hh:hh + 1, :])
                dp = dg(vc, gm[hh], NT)
                dsc = (pt * (dp - delta[hh:hh + 1, :])).astype(BF)
                dv = dv + dg(pt.astype(BF), gm[hh], NN)
                dk = dk + dg(dsc, qm[hh], NN)
                dq = dq + dg(dsc, km[hh][rows], TN)
            gqkv[1, rows, o] = dk.astype(BF)
            gqkv[2, rows, o] = dv.astype(BF)
        gqkv[0, :, o] = (dq * 0.125).astype(BF)

    pl.loop(0, 1)(attend)
    O.plane_one()
    U1.plane_two()
    D0.done()
    pl.loop(1, 2)(attend)
    U0.along()
    pl.loop(2, 3)(attend)
    D1.done()
    O.plane_two()

    def qkv_grad(part, first):
        @pl.loop(0, 3)
        def _(j):
            store(part, dg(tok[...], gqkv[j, :, first:first + hD], TN), ds(j * hD, hD))

    qkv_grad(A0, 0)
    A0.core()
    pl.loop(3, 4)(attend)
    A0.plane_one()
    U1.along()
    pl.loop(4, 5)(attend)
    U0.done()
    O.along()
    pl.loop(5, 6)(attend)
    wire.sent(A0.tc)
    qkv_grad(A1, hD)
    A1.core()
    for j in (0, 2):
        gvec[j:j + 1, :] = rows_sum(gqkv[j].astype(F32))
    tv = wire.send(gvec, vland.at[0], me.cdev)
    A0.plane_two()
    gmid[...] += dg(gqkv[0], w1[0], NT)
    A1.plane_one()
    gmid[...] += dg(gqkv[1], w1[1], NT)
    wire.recv(tv, vland.at[0])
    vsend[0] = gvec[...] + vland[0]
    tv = wire.send(vsend.at[0], vland.at[1], me.xdev)
    U1.done()
    gin = gattn
    gin[...] = (gmid[...] + dg(gqkv[2], w1[2], NT)).astype(BF)
    l_gin = local.start(gin.at[ds(z * Q, Q)], gin_out.at[z])
    t_gin = [wire.send(gin.at[ds(me.zidx[k] * Q, Q)], gin_out.at[z], me.zdev[k]) for k in range(3)]
    A0.along()
    O.done()
    wire.recv(tv, vland.at[1])
    vsend[1] = vsend[0] + vland[1]
    tv = wire.send(vsend.at[1], vland.at[2], me.ydev)
    A1.plane_two()
    A0.done()
    wire.recv(tv, vland.at[2])
    vsend[2] = vsend[1] + vland[2]
    tvs = [wire.send(vsend.at[2], vland.at[3 + k], me.zdev[k]) for k in range(3)]
    A1.along()
    total = vsend[2]
    for k in range(3):
        wire.recv(tvs[k], vland.at[3 + k])
        total = total + vland[3 + k]
    vsend[3] = total

    def exact(v, m):
        a = v.astype(BF)
        v = v - a.astype(F32)
        e = v.astype(BF)
        v = (v - e.astype(F32)).astype(BF)
        return dg(a, m, NT) + dg(e, m, NT) + dg(v, m, NT)

    per_row = D // (4 * r)
    gv = exact(total, place_matrix(128, D, me.k * r, r))
    row = vsend[3, pl.ds(ROW_UP + me.k // per_row, 1), :]
    gu = exact(jnp.broadcast_to(row, (VROWS, D)), place_matrix(128, D, (me.k % per_row) * (4 * r), 4 * r))
    ri = lax.broadcasted_iota(jnp.int32, (VROWS, 128), 0)
    gv_out[...] = jnp.where(ri < ROW_UP, gv, gu)
    A1.done()
    for k in range(3):
        wire.recv(t_out[k], bout.at[me.zfrom[k]])
        wire.recv(t_gin[k], gin_out.at[me.zfrom[k]])
    wire.finish()
    local.finish()


def per_device(fold, hidden_in, segment_ids, pad_mask, cotangent, w_query, bias_query, w_key, w_value, bias_value,
               w_out, bias_out, gain_attn, shift_attn, w_up, bias_up, w_down, bias_down, gain_ffn, shift_ffn):
    rows, Q, D = hidden_in.shape
    T = segment_ids.shape[1]
    mats = [w_query, w_key, w_value, w_out, w_up, w_down]
    vecs = [bias_query, bias_value, bias_out, gain_attn, shift_attn, bias_down, gain_ffn, shift_ffn, bias_up]
    hi = lax.axis_index("batch") // fold
    part = hi * 4 + lax.axis_index("seq")
    if fold > 1:
        def widen(w):
            whole = lax.all_gather(w, ("batch", "seq"), axis=0, tiled=True)
            n = w.shape[0] * fold
            return lax.dynamic_slice_in_dim(whole, part * n, n, 0)
        mats = [widen(w) for w in mats]
        vecs = [widen(v) for v in vecs]
    wq, wk, wv, wo, wu, wd = mats
    r, rd, FF = wq.shape[0], wd.shape[0], wu.shape[1]
    order = [vecs[0], jnp.zeros_like(vecs[0])] + vecs[1:8]
    table = jnp.stack([jnp.pad(v, (0, 128 - r)) for v in order] + [jnp.pad(vecs[8], (0, 128 - 4 * r))])
    table = jnp.pad(table, ((0, VROWS - table.shape[0]), (0, 0)))

    def shape(s, d=BF):
        return jax.ShapeDtypeStruct(s, d)

    any_spec = pl.BlockSpec(memory_space=ANY)
    vm_spec = pl.BlockSpec(memory_space=VMEM)
    saved = [shape((T, D)), shape((3, T, D)), shape((T, D)), shape((6, 8, T), F32), shape((T, D)), shape((T, D), F32),
             shape((T, 128), F32), shape((T, FF)), shape((T, FF)), shape((T, D), F32), shape((T, D)), shape((T, D)),
             shape((VROWS, D), F32), shape((VROWS, D), F32), shape((4, D, D)), shape((D, FF)), shape((4, D, D))]
    n_remote = 96
    fwd = pl.pallas_call(
        lambda *refs: forward_kernel(fold, T, D, FF, r, rd, *refs),
        name="forward",
        out_shape=saved,
        in_specs=[any_spec, any_spec, vm_spec, vm_spec] + [any_spec] * 6 + [vm_spec],
        out_specs=[any_spec] * len(saved),
        scratch_shapes=[
            VMEM((4, 4, r, D), BF), VMEM((4, r, FF), BF), VMEM((4, D, D), BF), VMEM((D, FF), BF), VMEM((4, D, D), BF),
            VMEM((T, D), BF), VMEM((T, D), BF), VMEM((3, T, D), BF), VMEM((T, D), BF), VMEM((6, 8, T), F32),
            VMEM((T, D), BF), VMEM((T, D), F32), VMEM((T, 128), F32), VMEM((T, D), F32), VMEM((T, FF), BF),
            VMEM((T, FF), BF), VMEM((T, D), F32), VMEM((T, D), BF), VMEM((T, D), BF),
            VMEM((VROWS, D), F32), VMEM((VROWS, D), F32), VMEM((4, VROWS, D), BF), VMEM((6, VROWS, D), BF),
            pltpu.SemaphoreType.DMA((n_remote,)), pltpu.SemaphoreType.DMA((n_remote,)), pltpu.SemaphoreType.DMA((32,)),
        ],
        compiler_params=pltpu.CompilerParams(collective_id=0, has_side_effects=True, vmem_limit_bytes=58 * 2**20),
    )
    kept = fwd(hidden_in, cotangent, segment_ids, pad_mask, wq, wk, wv, wo, wu, wd, table)

    first = D // 3
    hF, hA = FF // 2, 3 * D // 2
    cols = [(4 * rd, first), (4 * rd, D - first), (4 * r, hF), (4 * r, hF), (4 * r, D), (4 * r, hA), (4 * r, hA)]

    def bufs(f):
        return [VMEM(f(n, w), BF) for n, w in cols]

    four = [VMEM((2, 2, n, w), BF) for n, w in (cols[0], cols[1], cols[2], cols[4], cols[5])]
    bwd = pl.pallas_call(
        lambda *refs: backward_kernel(fold, T, D, FF, r, rd, [first], *refs),
        name="backward",
        out_shape=[shape((rows, Q, D)), shape((rows, Q, D)), shape((4, r, D), F32), shape((r, FF), F32), shape((rd, D), F32),
                   shape((VROWS, 128), F32)],
        in_specs=[vm_spec, vm_spec] + [any_spec] * len(saved),
        out_specs=[any_spec, any_spec, vm_spec, vm_spec, vm_spec, vm_spec],
        scratch_shapes=[
            VMEM((4, D, D), BF), VMEM((D, FF), BF), VMEM((T, D), BF), VMEM((3, T, D), BF), VMEM((T, D), BF),
            VMEM((6, 8, T), F32), VMEM((T, D), BF), VMEM((T, D), F32), VMEM((T, 128), F32), VMEM((T, FF), BF),
            VMEM((T, FF), BF), VMEM((T, D), F32), VMEM((T, D), BF), VMEM((VROWS, D), F32), VMEM((VROWS, D), F32),
            VMEM((T, D), BF), VMEM((T, D), BF), VMEM((3, T, D), BF),
        ] + four + bufs(lambda n, w: (2, 2, n, w)) + bufs(lambda n, w: (2, 2, n, w))
        + bufs(lambda n, w: (2, 2, n // 2, w)) + bufs(lambda n, w: (2, n // 2, w))
        + bufs(lambda n, w: (4, n // 4, w)) + bufs(lambda n, w: (3, n // 4, w)) + [
            VMEM((4, VROWS, D), F32), VMEM((6, VROWS, D), F32),
            pltpu.SemaphoreType.DMA((n_remote,)), pltpu.SemaphoreType.DMA((n_remote,)), pltpu.SemaphoreType.DMA((32,)),
        ],
        compiler_params=pltpu.CompilerParams(collective_id=1, has_side_effects=True, vmem_limit_bytes=60 * 2**20),
    )
    block_out, grad_in, gA, gU, gD, gv = bwd(segment_ids, pad_mask, *kept)
    grads = [gA[0], gv[ROW_BQ, :r], gA[1], gA[2], gv[ROW_BV, :r], gA[3], gv[ROW_BO, :r], gv[ROW_GA, :r], gv[ROW_SA, :r],
             gU, gv[ROW_UP, :4 * r], gD, gv[ROW_BD, :r], gv[ROW_GF, :r], gv[ROW_SF, :r]]
    if fold > 1:
        def narrow(g):
            n = g.shape[0]
            whole = jnp.zeros((32 * n,) + g.shape[1:], F32)
            whole = lax.dynamic_update_slice_in_dim(whole, g, part * n, 0)
            return lax.psum_scatter(whole, ("batch", "seq"), scatter_dimension=0, tiled=True)
        grads = [narrow(g) for g in grads]
    return (block_out, grad_in) + tuple(grads)


def solution(mesh):
    fold = mesh.shape["batch"] // 8
    mat, vec = P(("batch", "seq"), None), P(("batch", "seq"))
    act, rows = P("batch", "seq", None), P("batch", None)
    kinds = [mat, vec, mat, mat, vec, mat, vec, vec, vec, mat, vec, mat, vec, vec, vec]
    return jax.shard_map(
        lambda *args: per_device(fold, *args),
        mesh=mesh,
        in_specs=tuple([act, rows, rows, act] + kinds),
        out_specs=tuple([act, act] + kinds),
        check_vma=False,
    )
```

```python
import jax
import jax.numpy as jnp
from jax import lax
from jax.experimental import pallas as pl
from jax.experimental.pallas import tpu as pltpu
from jax.sharding import PartitionSpec as P

BF = jnp.bfloat16
F32 = jnp.float32
MESH = pl.DeviceIdType.MESH
EPS = 1e-5
NEG = -1e9
C0 = 0.7978845608028654
C1 = 0.044715
NN = (((1,), (0,)), ((), ()))
NT = (((1,), (1,)), ((), ()))
TN = (((0,), (0,)), ((), ()))
VMEM = pltpu.VMEM
ANY = pl.ANY
ROW_BQ, ROW_BV, ROW_BO, ROW_GA, ROW_SA, ROW_BD, ROW_GF, ROW_SF, ROW_UP = 0, 2, 3, 4, 5, 6, 7, 8, 9
VROWS = 16


def dg(a, b, dims):
    return lax.dot_general(a, b, dims, preferred_element_type=F32)


def ds(start, size):
    return pl.ds(pl.multiple_of(start, size), size)


class Place:
    def __init__(self, fold):
        bidx = lax.axis_index("batch")
        z = lax.axis_index("seq")
        hi = bidx // fold
        lo = bidx % fold
        y = hi // 4
        x = (hi // 2) % 2
        c = hi % 2
        self.y, self.x, self.c, self.z, self.b = y, x, c, z, hi
        self.k = hi * 4 + z
        self.bx = y * 4 + (1 - x) * 2 + c
        self.by = (1 - y) * 4 + x * 2 + c
        self.bd = (1 - y) * 4 + (1 - x) * 2 + c
        self.bc = y * 4 + x * 2 + (1 - c)

        def dev(block):
            return (block * fold + lo, z)

        self.xdev, self.ydev, self.cdev = dev(self.bx), dev(self.by), dev(self.bc)
        self.zidx = [z + 1 - 2 * (z % 2), z + 2 - 4 * (z // 2), 3 - z]
        self.zfrom = self.zidx
        self.zdev = [(bidx, zi) for zi in self.zidx]
        self.zp = z + 1 - 2 * (z % 2)
        self.inner = (z == 1) | (z == 2)
        self.outer = (z == 0) | (z == 3)
        self.zm = 3 - z
        self.pdev, self.mdev = (bidx, self.zp), (bidx, self.zm)

    def greet(self):
        bar = pltpu.get_barrier_semaphore()
        for d in [self.xdev, self.ydev, self.cdev] + self.zdev:
            pl.semaphore_signal(bar, inc=1, device_id=d, device_id_type=MESH)
        pl.semaphore_wait(bar, 6)


class Wire:
    def __init__(self, send_sems, recv_sems):
        self.ss, self.rs, self.n, self.open, self.cond = send_sems, recv_sems, 0, [], None

    def when(self, cond, body):
        @pl.when(cond)
        def _():
            self.cond = cond
            body()
            self.cond = None

    def send(self, src, dst, device):
        i = self.n
        self.n += 1

        def make():
            return pltpu.make_async_remote_copy(src_ref=src(), dst_ref=dst(), send_sem=self.ss.at[i], recv_sem=self.rs.at[i],
                                                device_id=device, device_id_type=MESH)

        make().start()
        tag = (i, device, make, self.cond)
        self.open.append(tag)
        return tag

    def recv(self, tag, dst):
        i, device = tag[:2]
        pltpu.make_async_remote_copy(src_ref=dst, dst_ref=dst, send_sem=self.ss.at[i], recv_sem=self.rs.at[i],
                                     device_id=device, device_id_type=MESH).wait_recv()

    def sent(self, tag):
        tag[2]().wait_send()
        self.open = [other for other in self.open if other is not tag]

    def finish(self):
        for tag in self.open:
            if tag[3] is None:
                tag[2]().wait_send()
            else:
                pl.when(tag[3])(lambda tag=tag: tag[2]().wait_send())
        self.open = []


class Local:
    def __init__(self, sems):
        self.sems, self.n, self.open = sems, 0, []

    def start(self, src, dst):
        i = self.n
        self.n += 1

        def make():
            return pltpu.make_async_copy(src(), dst(), self.sems.at[i])

        make().start()
        self.open.append(make)
        return make

    def wait(self, make):
        make().wait()
        self.open = [other for other in self.open if other is not make]

    def finish(self):
        for make in self.open:
            make().wait()
        self.open = []


def norm_rows(v, gain, shift):
    center = v - jnp.mean(v, axis=-1, keepdims=True)
    inv = lax.rsqrt(jnp.mean(center * center, axis=-1, keepdims=True) + EPS)
    xhat = center * inv
    return xhat * gain + shift, xhat, inv


def norm_back(g, xhat, inv, gain):
    e = g * gain
    return inv * (e - jnp.mean(e, axis=-1, keepdims=True) - xhat * jnp.mean(e * xhat, axis=-1, keepdims=True))


def rows_sum(v):
    return jnp.sum(v, axis=0, keepdims=True)


def place_matrix(rows, width, start, count):
    i = lax.broadcasted_iota(jnp.int32, (rows, width), 0)
    j = lax.broadcasted_iota(jnp.int32, (rows, width), 1)
    return jnp.where((j == start + i) & (i < count), 1.0, 0.0).astype(BF)


def segments(seg_ref, pad_ref, z, length):
    seg = seg_ref[pl.ds(z, 1), :].astype(F32)
    live = pad_ref[pl.ds(z, 1), :]
    keyed = jnp.where(live == 1, seg, -1.0)

    def column(row):
        return jnp.broadcast_to(row, (128, length)).T[:, 0:1]

    return seg, keyed, column


def forward_kernel(fold, T, D, FF, r, rd,
                   hidden, cot, seg, pad, wq, wk, wv, wo, wu, wd,
                   v0, v1, v2, v3, v4, v5, v6, v7, v8,
                   o_tok, o_qkv, o_att, o_lse, o_nlow, o_xh1, o_inv1, o_act, o_gp, o_gmid, o_gffn, o_out, o_vec,
                   o_gvec, o_wA, o_wU, o_wD,
                   zA, zU, wA, wU, wD, tok, cotr, qkv, att, lse, nlow, xh1, inv1, normed, act, gp, tmp, gffn, out,
                   vec, gvec, table, vsend, vland, ss, rs, ls):
    me = Place(fold)
    wire = Wire(ss, rs)
    local = Local(ls)
    z, b = me.z, me.b
    Q = T // 4
    block, dblock = 4 * r, 4 * rd

    def drow(k, sub):
        return wD.at[k // 2, ds((k % 2) * dblock + sub * rd, rd)]

    def dhalf(k, sub, cols):
        return wD.at[k // 2, ds((k % 2) * dblock + sub * rd, rd), cols]

    own = [local.start(lambda w=w: w, lambda i=i: zA.at[i, z]) for i, w in enumerate((wq, wk, wv, wo))]
    own_u = local.start(lambda: wu, lambda: zU.at[z])
    own_d = local.start(lambda: wd, lambda: drow(b, z))
    own_t = local.start(lambda: hidden.at[z], lambda: tok.at[ds(z * Q, Q)])
    own_c = local.start(lambda: cot.at[z], lambda: cotr.at[ds(z * Q, Q)])

    table[...] = jnp.zeros_like(table)
    for i, ref in zip((ROW_BQ, ROW_BV, ROW_BO, ROW_GA, ROW_SA, ROW_BD, ROW_GF, ROW_SF, ROW_UP), (v0, v1, v2, v3, v4, v5, v6, v7, v8)):
        table[i:i + 1, 0:ref.shape[1]] = ref[...].astype(F32)
    given = table[...].astype(BF)
    v_a = dg(given, place_matrix(128, D, me.k * r, r), NN)
    per_row = D // block
    v_u = dg(given, place_matrix(128, D, (me.k % per_row) * block, block), NN)[ROW_UP:ROW_UP + 1]
    ri = lax.broadcasted_iota(jnp.int32, (VROWS, D), 0)
    up_row = ROW_UP + me.k // per_row
    vsend[0] = jnp.where(ri < ROW_UP, v_a, jnp.where(ri == up_row, jnp.broadcast_to(v_u, (VROWS, D)), 0.0)).astype(BF)

    me.greet()

    def zsend(src, dst):
        return [wire.send(lambda k=k: src(k), dst, me.zdev[k]) for k in range(3)]

    def zrecv(tags, dst):
        for k in range(3):
            wire.recv(tags[k], dst(k))

    class Spread:
        def __init__(self, region):
            self.region = region

        def go(self, k, half, n, device):
            return wire.send(lambda: self.region(k, half, n), lambda: self.region(k, half, n), device)

        def own(self):
            self.tx = self.go(b, 0, 2, me.xdev)
            self.ty = self.go(b, 0, 2, me.ydev)
            self.tc = [self.go(b, 0, 2, me.cdev)]

        def mid(self):
            g = self.region
            wire.recv(self.tx, g(me.bx, 0, 2))
            self.f1 = self.go(me.bx, 0, 1, me.ydev)
            wire.recv(self.ty, g(me.by, 0, 2))
            self.f2 = self.go(me.by, 1, 1, me.xdev)
            self.tc.append(self.go(me.bx, 0, 2, me.cdev))
            self.tc.append(self.go(me.by, 0, 2, me.cdev))

        def last(self):
            g = self.region
            wire.recv(self.f1, g(me.bd, 0, 1))
            wire.recv(self.f2, g(me.bd, 1, 1))
            self.tc.append(self.go(me.bd, 0, 2, me.cdev))

        def done(self):
            for tag, k in zip(self.tc, (me.b, me.bx, me.by, me.bd)):
                wire.recv(tag, self.region(k + 1 - 2 * me.c, 0, 2))

    def part(k, half, n, size):
        h = size // 2
        return ds(k * size + half * h, h) if n == 1 else ds(k * size, size)

    hF, hD = FF // 2, D // 2
    s_qkv = Spread(lambda k, half, n: wA.at[0:3, part(k, half, n, block)])
    s_o = Spread(lambda k, half, n: wA.at[3, part(k, half, n, block)])
    s_u = [Spread(lambda k, half, n, i=i: wU.at[part(k, half, n, block), i * hF:(i + 1) * hF]) for i in range(2)]
    s_d = [Spread(lambda k, half, n, i=i: wD.at[k // 2, part(k % 2, half, n, dblock), i * hD:(i + 1) * hD]) for i in range(2)]


    def join(parts):
        return jnp.concatenate([p.astype(F32) for p in parts], axis=0).astype(BF)

    t_vec = [wire.send(lambda: vsend.at[0], lambda k=k: vland.at[k], me.zdev[k]) for k in range(3)]
    for cp in own[:3]:
        local.wait(cp)
    t_qkv = zsend(lambda k: zA.at[0:3, z], lambda: zA.at[0:3, z])
    t_u = zsend(lambda k: wu, lambda: zU.at[z])
    t_hid = zsend(lambda k: hidden.at[me.zidx[k]], lambda: tok.at[ds(z * Q, Q)])
    local.wait(own[3])
    t_o = zsend(lambda k: zA.at[3, z], lambda: zA.at[3, z])
    halves = [slice(0, hD), slice(hD, D)]
    t_d = [zsend(lambda k, h=h: wd.at[:, h], lambda h=h: dhalf(b, z, h)) for h in halves]

    zrecv(t_vec, lambda k: vland.at[k])
    vsend[1] = vsend[0] + vland[0] + vland[1] + vland[2]
    tv = wire.send(lambda: vsend.at[1], lambda: vland.at[3], me.xdev)

    zrecv(t_qkv, lambda k: zA.at[0:3, me.zfrom[k]])
    for i in range(3):
        wA[i, ds(b * block, block), :] = join([zA[i, s] for s in range(4)])
    s_qkv.own()
    wire.recv(tv, vland.at[3])
    vsend[2] = vsend[1] + vland[3]
    tv = wire.send(lambda: vsend.at[2], lambda: vland.at[4], me.ydev)
    s_qkv.mid()
    wire.recv(tv, vland.at[4])
    vsend[3] = vsend[2] + vland[4]
    tv = wire.send(lambda: vsend.at[3], lambda: vland.at[5], me.cdev)
    local.wait(own_u)
    zrecv(t_u, lambda k: zU.at[me.zfrom[k]])
    wU[ds(b * block, block), :] = join([zU[s] for s in range(4)])
    s_u[0].own()
    s_u[1].own()
    s_qkv.last()
    wire.recv(tv, vland.at[5])
    vec[...] = vsend[3].astype(F32) + vland[5].astype(F32)
    local.start(lambda: vec, lambda: o_vec)
    s_qkv.done()
    s_u[0].mid()
    local.wait(own_t)
    zrecv(t_hid, lambda k: tok.at[ds(me.zfrom[k] * Q, Q)])
    local.start(lambda: tok, lambda: o_tok)

    def project(j):
        v = dg(tok[...], wA[j], NN) + vec[pl.ds(j, 1), :]
        v = v.astype(BF)
        qkv[j] = v * jnp.where(j == 0, 0.125, 1.0).astype(BF)

    pl.loop(0, 3)(project)
    local.start(lambda: qkv, lambda: o_qkv)
    s_u[1].mid()
    zrecv(t_o, lambda k: zA.at[3, me.zfrom[k]])
    wA[3, ds(b * block, block), :] = join([zA[3, s] for s in range(4)])
    s_o.own()

    seg_row, key_row, column = segments(seg, pad, z, T)
    seg_col = column(seg_row)
    lane = lax.broadcasted_iota(jnp.int32, (T, 128), 1)
    lo = lane < 64

    def attend(p):
        o = ds(p * 128, 128)
        k = qkv[1, :, o]
        v = qkv[2, :, o]
        one = jnp.ones_like(v)
        zero = jnp.zeros_like(v)
        v0_, v1_ = jnp.where(lo, v, one), jnp.where(lo, one, v)
        k0, k1 = jnp.where(lo, k, zero), jnp.where(lo, zero, k)
        for step in range(T // 128):
            rows = slice(step * 128, (step + 1) * 128)
            q = qkv[0, rows, o]
            ok = seg_col[rows] == key_row
            res, top = [], []
            for kk, vv in ((k0, v0_), (k1, v1_)):
                s = jnp.where(ok, dg(q, kk, NT), NEG)
                m = jnp.max(s, axis=-1, keepdims=True)
                res.append(dg(jnp.exp(s - m).astype(BF), vv, NN))
                top.append(m)
            low = lo[:128]
            num = jnp.where(low, res[0], res[1])
            den = pltpu.roll(jnp.where(low, res[1], res[0]), 64, 1)
            att[rows, o] = (num / den).astype(BF)
            lt = (jnp.log(den) + jnp.where(low, top[0], top[1])).T
            lse[p, 0:1, rows] = lt[0:1]
            lse[p, 1:2, rows] = lt[64:65]

    tags = {}

    def serve0():
        s_u[0].last()

    def serve1():
        pass

    def serve2():
        local.wait(own_d)
        zrecv(t_d[0], lambda k: dhalf(b, me.zfrom[k], halves[0]))
        s_d[0].own()
        s_o.mid()

    def serve3():
        s_u[1].last()

    def serve4():
        zrecv(t_d[1], lambda k: dhalf(b, me.zfrom[k], halves[1]))
        s_d[1].own()
        tags["cot"] = zsend(lambda k: cot.at[me.zidx[k]], lambda: cotr.at[ds(z * Q, Q)])
        s_o.last()

    def serve5():
        s_d[0].mid()

    services = [serve0, serve1, serve2, serve3, serve4, serve5]

    @pl.loop(0, 6)
    def _(p):
        attend(p)
        for i, service in enumerate(services):
            pl.when(p == i)(service)

    local.start(lambda: att, lambda: o_att)
    local.start(lambda: lse, lambda: o_lse)
    s_o.done()
    local.start(lambda: wA, lambda: o_wA)
    tmp[...] = dg(att[...], wA[3], NN) + vec[ROW_BO:ROW_BO + 1, :]

    def norm_one(i):
        rr = ds(i * 64, 64)
        y_, xh, inv = norm_rows(tmp[rr, :] + tok[rr, :].astype(F32), vec[ROW_GA:ROW_GA + 1, :], vec[ROW_SA:ROW_SA + 1, :])
        normed[rr, :] = y_
        nlow[rr, :] = y_.astype(BF)
        xh1[rr, :] = xh
        inv1[rr, :] = jnp.broadcast_to(inv, (64, 128))

    pl.loop(0, T // 64)(norm_one)
    local.start(lambda: nlow, lambda: o_nlow)
    local.start(lambda: xh1, lambda: o_xh1)
    local.start(lambda: inv1, lambda: o_inv1)
    s_u[0].done()
    s_u[1].done()
    local.start(lambda: wU, lambda: o_wU)

    wide = D // 2

    def up(j):
        o = ds(j * wide, wide)
        bias = vec[pl.ds(ROW_UP + j // 2, 1), ds((j % 2) * wide, wide)]
        v = dg(nlow[...], wU[:, o], NN) + bias
        v2 = v * v
        t = jnp.tanh(v * (C0 + C0 * C1 * v2))
        half = 0.5 * (1 + t)
        act[:, o] = (v * half).astype(BF)
        gp[:, o] = (half + 0.5 * v * (1 - t * t) * (C0 + 3 * C0 * C1 * v2)).astype(BF)

    @pl.loop(0, FF // wide)
    def _(j):
        up(j)
        pl.when(j == 2)(s_d[1].mid)

    local.start(lambda: act, lambda: o_act)
    local.start(lambda: gp, lambda: o_gp)
    s_d[0].last()
    s_d[1].last()
    s_d[0].done()
    s_d[1].done()
    local.start(lambda: wD, lambda: o_wD)

    tmp[...] = dg(act[:, 0:D], wD[0], NN) + vec[ROW_BD:ROW_BD + 1, :]

    def down(j):
        tmp[...] += dg(act[:, ds(j * D, D)], wD[j], NN)

    pl.loop(1, FF // D)(down)
    local.wait(own_c)
    zrecv(tags["cot"], lambda k: cotr.at[ds(me.zfrom[k] * Q, Q)])
    zero_row = jnp.zeros((1, D), F32)
    gvec[...] = jnp.zeros_like(gvec)

    def norm_two(i, sums):
        rr = ds(i * 64, 64)
        gain = vec[ROW_GF:ROW_GF + 1, :]
        y_, xh, inv = norm_rows(tmp[rr, :] + normed[rr, :], gain, vec[ROW_SF:ROW_SF + 1, :])
        out[rr, :] = y_.astype(BF)
        g = cotr[rr, :].astype(F32)
        gm = norm_back(g, xh, inv, gain)
        gl = gm.astype(BF)
        tmp[rr, :] = gm
        gffn[rr, :] = gl
        return sums[0] + rows_sum(g * xh), sums[1] + rows_sum(g), sums[2] + rows_sum(gl.astype(F32))

    s0, s1, s2 = lax.fori_loop(0, T // 64, norm_two, (zero_row, zero_row, zero_row))
    gvec[ROW_GF:ROW_GF + 1, :] = s0
    gvec[ROW_SF:ROW_SF + 1, :] = s1
    gvec[ROW_BD:ROW_BD + 1, :] = s2
    local.start(lambda: gffn, lambda: o_gffn)
    local.start(lambda: out, lambda: o_out)
    local.start(lambda: tmp, lambda: o_gmid)
    local.start(lambda: gvec, lambda: o_gvec)
    wire.finish()
    local.finish()


def backward_kernel(fold, T, D, FF, r, rd, refs):
    take = iter(refs)

    def some(n):
        return [next(take) for _ in range(n)]

    (seg, pad, i_tok, i_qkv, i_att, i_lse, i_nlow, i_xh1, i_inv1, i_act, i_gp, i_gmid, i_gffn, i_out,
     i_vec, i_gvec, i_wA, i_wU, i_wD) = some(19)
    bout, gin_out, gA_out, gU_out, gD_out, gv_out = some(6)
    (w1, wU, tok, qkv, att, lse, nlow, xh1, inv1, act, gp, gmid, gffn, vec, gvec, gattn, gatt, gqkv) = some(18)
    d_snd0, d_snd1, u_snd, o_snd, a_snd = some(5)
    mines, ones, firsts, seconds, outs, ins = [some(8) for _ in range(6)]
    vsend, vland, ss, rs, ls = some(5)

    me = Place(fold)
    wire = Wire(ss, rs)
    local = Local(ls)
    z, b, c, x, y = me.z, me.b, me.c, me.x, me.y
    Q = T // 4

    def load(src, dst):
        return local.start(lambda: src, lambda: dst)

    l_act, l_gffn, l_wD, l_gp = load(i_act, act), load(i_gffn, gffn), load(i_wD, w1), load(i_gp, gp)
    l_gvec, l_nlow, l_gmid, l_wU = load(i_gvec, gvec), load(i_nlow, nlow), load(i_gmid, gmid), load(i_wU, wU)
    l_vec, l_xh1, l_inv1, l_att = load(i_vec, vec), load(i_xh1, xh1), load(i_inv1, inv1), load(i_att, att)
    l_qkv, l_lse, l_tok = load(i_qkv, qkv), load(i_lse, lse), load(i_tok, tok)
    local.start(lambda: i_out.at[ds(z * Q, Q)], lambda: bout.at[z])
    me.greet()
    t_out = [wire.send(lambda k=k: i_out.at[ds(me.zidx[k] * Q, Q)], lambda: bout.at[z], me.zdev[k]) for k in range(3)]

    def keep(v0, v1):
        first = c == 0
        return jnp.where(first, v0, v1).astype(BF), jnp.where(first, v1, v0).astype(BF)

    def plus(a, e):
        return (a.astype(F32) + e.astype(F32)).astype(BF)

    class Sum:
        def __init__(self, i, snd, rows, line, write):
            self.snd, self.rows, self.line, self.write = snd, rows, line, write
            self.mine, self.r1, self.ra, self.rb, self.zs, self.zr = (mines[i], ones[i], firsts[i], seconds[i], outs[i], ins[i])

        def core(self):
            self.tc = wire.send(lambda: self.snd, lambda: self.r1, me.cdev)

        def plane_one(self):
            n = 2 * self.rows
            wire.recv(self.tc, self.r1)

            @pl.loop(0, 2)
            def _(i):
                for j in range(2):
                    self.mine[i, j] = plus(self.mine[i, j], self.r1[i, j])

            self.tx = wire.send(lambda: self.mine.at[:, 1 - x, 0:n], lambda: self.ra.at[0], me.xdev)
            self.ty = wire.send(lambda: self.mine.at[1 - y, :, n:2 * n], lambda: self.ra.at[1], me.ydev)

        def plane_two(self):
            n = 2 * self.rows
            wire.recv(self.tx, self.ra.at[0])
            for i in range(2):
                self.mine[i, x, 0:n] = plus(self.mine[i, x, 0:n], self.ra[0, i])
            self.ty2 = wire.send(lambda: self.mine.at[1 - y, x, 0:n], lambda: self.rb.at[0], me.ydev)
            wire.recv(self.ty, self.ra.at[1])
            for i in range(2):
                self.mine[y, i, n:2 * n] = plus(self.mine[y, i, n:2 * n], self.ra[1, i])
            self.tx2 = wire.send(lambda: self.mine.at[y, 1 - x, n:2 * n], lambda: self.rb.at[1], me.xdev)

        def along(self):
            n = 2 * self.rows
            q = self.rows
            for half, tag in ((0, self.ty2), (1, self.tx2)):
                wire.recv(tag, self.rb.at[half])
                v = self.mine[y, x, half * n:(half + 1) * n].astype(F32) + self.rb[half].astype(F32)
                self.zs[2 * half] = v[0:q].astype(BF)
                self.zs[2 * half + 1] = v[q:2 * q].astype(BF)
            if self.line:
                def outer():
                    self.t1 = wire.send(lambda: self.zs.at[pl.ds(jnp.where(z == 0, 1, 0), 3)], lambda: self.zr.at[0:3], me.pdev)

                wire.when(me.outer, outer)
            else:
                self.tz = [wire.send(lambda k=k: self.zs.at[me.zidx[k]], lambda k=k: self.zr.at[k], me.zdev[k]) for k in range(3)]

        def line_one(self):
            def inner():
                wire.recv(self.t1, self.zr.at[0:3])
                base = jnp.where(z == 1, 1, 0)
                start = jnp.where(z == 1, 2, 0)
                for i in range(2):
                    self.zs[start + i] = plus(self.zs[start + i], self.zr[start + i - base])
                self.t2 = wire.send(lambda: self.zs.at[pl.ds(jnp.where(z == 1, 2, 0), 2)], lambda: self.zr.at[3:5], me.mdev)

            wire.when(me.inner, inner)

        def line_two(self):
            def inner():
                wire.recv(self.t2, self.zr.at[3:5])
                base = jnp.where(z == 1, 1, 0)
                pair = jnp.where(z == 1, 0, 2)
                self.zs[me.zp] = plus(self.zs[me.zp], self.zr[3 + me.zp - pair])
                self.t3 = wire.send(lambda: self.zs.at[me.zp], lambda: self.zr.at[0], me.pdev)
                self.write(self.zs[z].astype(F32) + self.zr[z - base].astype(F32) + self.zr[3 + z - pair].astype(F32))

            wire.when(me.inner, inner)

        def done(self):
            if self.line:
                def outer():
                    wire.recv(self.t3, self.zr.at[0])
                    self.write(self.zs[z].astype(F32) + self.zr[0].astype(F32))

                wire.when(me.outer, outer)
            else:
                v = self.zs[z].astype(F32)
                for k in range(3):
                    wire.recv(self.tz[k], self.zr.at[k])
                    v = v + self.zr[k].astype(F32)
                self.write(v)

    third, hF, hD = D // 3, FF // 2, D // 2

    def write_d(i):
        def f(v):
            gD_out[:, i * third:(i + 1) * third] = v
        return f

    def write_u(i):
        def f(v):
            gU_out[:, i * hF:(i + 1) * hF] = v
        return f

    def write_o(v):
        gA_out[3] = v

    def write_a(i):
        def f(v):
            for m in range(3):
                gA_out[m, :, i * hD:(i + 1) * hD] = v[:, m * hD:(m + 1) * hD]
        return f

    D0 = Sum(0, d_snd0, rd, False, write_d(0))
    D1 = Sum(1, d_snd1, rd, False, write_d(1))
    D2 = Sum(2, d_snd0, rd, False, write_d(2))
    U0 = Sum(3, u_snd, r, False, write_u(0))
    U1 = Sum(4, u_snd, r, True, write_u(1))
    O = Sum(5, o_snd, r, False, write_o)
    A0 = Sum(6, a_snd, r, False, write_a(0))
    A1 = Sum(7, a_snd, r, False, write_a(1))

    def down_grad(part, i):
        cols = slice(i * third, (i + 1) * third)

        @pl.loop(0, 4)
        def _(i):
            v = dg(act[:, ds(i * D, D)], gffn[:, cols], TN)
            mine, theirs = keep(v[0:4 * rd], v[4 * rd:8 * rd])
            part.mine[i // 2, i % 2] = mine
            part.snd[i // 2, i % 2] = theirs

    def store(part, v, cols):
        n = 4 * r
        for i in range(4):
            mine, theirs = keep(v[(2 * i) * n:(2 * i + 1) * n], v[(2 * i + 1) * n:(2 * i + 2) * n])
            part.mine[i // 2, i % 2, :, cols] = mine
            part.snd[i // 2, i % 2, :, cols] = theirs

    def inner(j):
        o = ds(j * D, D)
        gi = (dg(gffn[...], w1[j], NT) * gp[:, o].astype(F32)).astype(BF)
        gp[:, o] = gi
        gvec[pl.ds(ROW_UP + j, 1), :] = rows_sum(gi.astype(F32))

    def up_grad(part, first):
        wide = hF // 3

        @pl.loop(0, 3)
        def _(j):
            o = ds(j * wide, wide)
            store(part, dg(nlow[...], gp[:, ds(first + j * wide, wide)], TN), o)

    local.wait(l_act)
    local.wait(l_gffn)
    down_grad(D0, 0)
    D0.core()
    down_grad(D1, 1)
    D1.core()
    D0.plane_one()
    wire.sent(D0.tc)
    down_grad(D2, 2)
    D2.core()
    D1.plane_one()
    local.wait(l_wD)
    local.wait(l_gp)
    local.wait(l_gvec)
    pl.loop(0, FF // D)(inner)
    l_wA = load(i_wA, w1)
    D0.plane_two()
    D2.plane_one()
    local.wait(l_wU)
    local.wait(l_gmid)
    gmid[...] += dg(gp[...], wU[...], NT)
    local.wait(l_vec)
    local.wait(l_xh1)
    local.wait(l_inv1)
    zero_row = jnp.zeros((1, D), F32)

    def norm_one(i, sums):
        rr = ds(i * 64, 64)
        g = gmid[rr, :]
        xh = xh1[rr, :]
        gm = norm_back(g, xh, inv1[rr, 0:1], vec[ROW_GA:ROW_GA + 1, :])
        gl = gm.astype(BF)
        gmid[rr, :] = gm
        gattn[rr, :] = gl
        return sums[0] + rows_sum(g * xh), sums[1] + rows_sum(g), sums[2] + rows_sum(gl.astype(F32))

    s0, s1, s2 = lax.fori_loop(0, T // 64, norm_one, (zero_row, zero_row, zero_row))
    gvec[ROW_GA:ROW_GA + 1, :] = s0
    gvec[ROW_SA:ROW_SA + 1, :] = s1
    gvec[ROW_BO:ROW_BO + 1, :] = s2
    D1.plane_two()
    local.wait(l_nlow)
    up_grad(U0, 0)
    U0.core()
    local.wait(l_att)
    local.wait(l_wA)
    gatt[...] = dg(gattn[...], w1[3], NT).astype(BF)
    local.wait(l_qkv)
    local.wait(l_lse)
    local.wait(l_tok)

    seg_row, key_row, column = segments(seg, pad, z, T)
    key_col = column(key_row)
    lane = lax.broadcasted_iota(jnp.int32, (T, 128), 1)
    lo = lane < 64
    pick = (lax.broadcasted_iota(jnp.int32, (8, 128), 1) // 64 == lax.broadcasted_iota(jnp.int32, (8, 128), 0)).astype(BF)

    def attend(p):
        o = ds(p * 128, 128)
        q = qkv[0, :, o]
        k = qkv[1, :, o]
        g = gatt[:, o]
        prod = g.astype(F32) * att[:, o].astype(F32)
        hi = prod.astype(BF)
        rest = (prod - hi.astype(F32)).astype(BF)
        delta = dg(pick, hi, NT) + dg(pick, rest, NT)
        zero = jnp.zeros_like(q)
        qm = (jnp.where(lo, q, zero), jnp.where(lo, zero, q))
        gm = (jnp.where(lo, g, zero), jnp.where(lo, zero, g))
        km = (jnp.where(lo, k, zero), jnp.where(lo, zero, k))
        dq = jnp.zeros((T, 128), F32)
        for step in range(T // 128):
            rows = slice(step * 128, (step + 1) * 128)
            kc = qkv[1, rows, o]
            vc = qkv[2, rows, o]
            ok = key_col[rows] == seg_row
            dk = jnp.zeros((128, 128), F32)
            dv = jnp.zeros((128, 128), F32)
            for hh in range(2):
                s = jnp.where(ok, dg(kc, qm[hh], NT), NEG)
                pt = jnp.exp(s - lse[p, hh:hh + 1, :])
                dp = dg(vc, gm[hh], NT)
                dsc = (pt * (dp - delta[hh:hh + 1, :])).astype(BF)
                dv = dv + dg(pt.astype(BF), gm[hh], NN)
                dk = dk + dg(dsc, qm[hh], NN)
                dq = dq + dg(dsc, km[hh][rows], TN)
            gqkv[1, rows, o] = dk.astype(BF)
            gqkv[2, rows, o] = dv.astype(BF)
        gqkv[0, :, o] = (dq * 0.125).astype(BF)

    def qkv_grad(part, first):
        @pl.loop(0, 3)
        def _(j):
            store(part, dg(tok[...], gqkv[j, :, first:first + hD], TN), ds(j * hD, hD))

    def serve0():
        U0.plane_one()
        D2.plane_two()
        D0.along()

    def serve1():
        D1.along()
        wire.sent(U0.tc)
        up_grad(U1, hF)
        U1.core()

    def serve2():
        U1.plane_one()
        D0.done()

    def serve3():
        U0.plane_two()

    def serve4():
        D1.done()
        D2.along()

    def serve5():
        U1.plane_two()

    services = [serve0, serve1, serve2, serve3, serve4, serve5]

    @pl.loop(0, 6)
    def _(p):
        attend(p)
        for i, service in enumerate(services):
            pl.when(p == i)(service)

    gin = gattn
    store(O, dg(att[...], gattn[...], TN), slice(0, D))
    O.core()
    U0.along()
    gmid[...] += dg(gqkv[0], w1[0], NT)
    gmid[...] += dg(gqkv[1], w1[1], NT)
    gin[...] = (gmid[...] + dg(gqkv[2], w1[2], NT)).astype(BF)
    local.start(lambda: gin.at[ds(z * Q, Q)], lambda: gin_out.at[z])
    t_gin = [wire.send(lambda k=k: gin.at[ds(me.zidx[k] * Q, Q)], lambda: gin_out.at[z], me.zdev[k]) for k in range(3)]
    O.plane_one()
    qkv_grad(A0, 0)
    A0.core()
    for j, row in ((0, ROW_BQ), (2, ROW_BV)):
        gvec[row:row + 1, :] = rows_sum(gqkv[j].astype(F32))
    tv = wire.send(lambda: gvec, lambda: vland.at[0], me.cdev)
    A0.plane_one()
    wire.sent(A0.tc)
    qkv_grad(A1, hD)
    A1.core()
    D2.done()
    wire.recv(tv, vland.at[0])
    vsend[0] = gvec[...] + vland[0]
    tv = wire.send(lambda: vsend.at[0], lambda: vland.at[1], me.xdev)
    O.plane_two()
    U1.along()
    A1.plane_one()
    wire.recv(tv, vland.at[1])
    vsend[1] = vsend[0] + vland[1]
    tv = wire.send(lambda: vsend.at[1], lambda: vland.at[2], me.ydev)
    A0.plane_two()
    O.along()
    wire.recv(tv, vland.at[2])
    vsend[2] = vsend[1] + vland[2]
    tvs = [wire.send(lambda: vsend.at[2], lambda k=k: vland.at[3 + k], me.zdev[k]) for k in range(3)]
    A1.plane_two()
    U1.line_one()
    A0.along()
    A1.along()
    U0.done()
    U1.line_two()
    U1.done()
    O.done()
    total = vsend[2]
    for k in range(3):
        wire.recv(tvs[k], vland.at[3 + k])
        total = total + vland[3 + k]
    vsend[3] = total

    def exact(v, m):
        a = v.astype(BF)
        v = v - a.astype(F32)
        e = v.astype(BF)
        v = (v - e.astype(F32)).astype(BF)
        return dg(a, m, NT) + dg(e, m, NT) + dg(v, m, NT)

    per_row = D // (4 * r)
    gv = exact(total, place_matrix(128, D, me.k * r, r))
    row = vsend[3, pl.ds(ROW_UP + me.k // per_row, 1), :]
    gu = exact(jnp.broadcast_to(row, (VROWS, D)), place_matrix(128, D, (me.k % per_row) * (4 * r), 4 * r))
    ri = lax.broadcasted_iota(jnp.int32, (VROWS, 128), 0)
    gv_out[...] = jnp.where(ri < ROW_UP, gv, gu)
    A0.done()
    A1.done()
    for k in range(3):
        wire.recv(t_out[k], bout.at[me.zfrom[k]])
        wire.recv(t_gin[k], gin_out.at[me.zfrom[k]])
    wire.finish()
    local.finish()


def finish_kernel(bout, gin, gA, gU, gD, gv, o_b, o_g, o_q, o_k, o_v, o_o, o_u, o_d, *rest):
    vecs, (s_b, s_g, s_A, s_U, s_D, sems) = rest[:9], rest[9:]
    loads = [(bout, s_b), (gin, s_g), (gA, s_A), (gU, s_U), (gD, s_D)]
    loads = [pltpu.make_async_copy(src, dst, sems.at[i]) for i, (src, dst) in enumerate(loads)]
    for cp in loads:
        cp.start()
    for row, ref in zip((ROW_BQ, ROW_BV, ROW_BO, ROW_GA, ROW_SA, ROW_UP, ROW_BD, ROW_GF, ROW_SF), vecs):
        ref[...] = gv[row:row + 1, 0:ref.shape[1]]
    stores = [[(s_b, o_b)], [(s_g, o_g)], [(s_A.at[i], ref) for i, ref in enumerate((o_q, o_k, o_v, o_o))], [(s_U, o_u)], [(s_D, o_d)]]
    out, n = [], len(loads)
    for cp, group in zip(loads, stores):
        cp.wait()
        for src, dst in group:
            out.append(pltpu.make_async_copy(src, dst, sems.at[n]))
            out[-1].start()
            n += 1
    for cp in out:
        cp.wait()


def per_device(fold, hidden_in, segment_ids, pad_mask, cotangent, w_query, bias_query, w_key, w_value, bias_value,
               w_out, bias_out, gain_attn, shift_attn, w_up, bias_up, w_down, bias_down, gain_ffn, shift_ffn):
    rows, Q, D = hidden_in.shape
    T = segment_ids.shape[1]
    mats = [w_query, w_key, w_value, w_out, w_up, w_down]
    vecs = [bias_query, bias_value, bias_out, gain_attn, shift_attn, bias_down, gain_ffn, shift_ffn, bias_up]
    hi = lax.axis_index("batch") // fold
    part = hi * 4 + lax.axis_index("seq")
    if fold > 1:
        def widen(w):
            whole = lax.all_gather(w, ("batch", "seq"), axis=0, tiled=True)
            n = w.shape[0] * fold
            return lax.dynamic_slice_in_dim(whole, part * n, n, 0)
        mats = [widen(w) for w in mats]
        vecs = [widen(v) for v in vecs]
    wq, wk, wv, wo, wu, wd = mats
    r, rd, FF = wq.shape[0], wd.shape[0], wu.shape[1]

    def shape(s, d=BF):
        return jax.ShapeDtypeStruct(s, d)

    any_spec = pl.BlockSpec(memory_space=ANY)
    vm_spec = pl.BlockSpec(memory_space=VMEM)
    saved = [shape((T, D)), shape((3, T, D)), shape((T, D)), shape((6, 8, T), F32), shape((T, D)), shape((T, D), F32),
             shape((T, 128), F32), shape((T, FF)), shape((T, FF)), shape((T, D), F32), shape((T, D)), shape((T, D)),
             shape((VROWS, D), F32), shape((VROWS, D), F32), shape((4, D, D)), shape((D, FF)), shape((4, D, D))]
    n_remote = 112
    sems = [pltpu.SemaphoreType.DMA((n_remote,)), pltpu.SemaphoreType.DMA((n_remote,)), pltpu.SemaphoreType.DMA((32,))]
    fwd = pl.pallas_call(
        lambda *refs: forward_kernel(fold, T, D, FF, r, rd, *refs),
        name="forward",
        out_shape=saved,
        in_specs=[any_spec, any_spec, vm_spec, vm_spec] + [any_spec] * 6 + [vm_spec] * 9,
        out_specs=[any_spec] * len(saved),
        scratch_shapes=[
            VMEM((4, 4, r, D), BF), VMEM((4, r, FF), BF), VMEM((4, D, D), BF), VMEM((D, FF), BF), VMEM((4, D, D), BF),
            VMEM((T, D), BF), VMEM((T, D), BF), VMEM((3, T, D), BF), VMEM((T, D), BF), VMEM((6, 8, T), F32),
            VMEM((T, D), BF), VMEM((T, D), F32), VMEM((T, 128), F32), VMEM((T, D), F32), VMEM((T, FF), BF),
            VMEM((T, FF), BF), VMEM((T, D), F32), VMEM((T, D), BF), VMEM((T, D), BF),
            VMEM((VROWS, D), F32), VMEM((VROWS, D), F32), VMEM((VROWS, 128), F32), VMEM((4, VROWS, D), BF),
            VMEM((6, VROWS, D), BF),
        ] + sems,
        compiler_params=pltpu.CompilerParams(collective_id=0, has_side_effects=True, vmem_limit_bytes=58 * 2**20),
    )
    kept = fwd(hidden_in, cotangent, segment_ids, pad_mask, wq, wk, wv, wo, wu, wd, *[v.reshape(1, -1) for v in vecs])

    parts = [(4 * rd, D // 3, False)] * 3 + [(4 * r, FF // 2, False), (4 * r, FF // 2, True)] + [(4 * r, D, False)] + [(4 * r, 3 * D // 2, False)] * 2

    def bufs(f):
        return [VMEM(f(n, w, line), BF) for n, w, line in parts]

    bwd = pl.pallas_call(
        lambda *refs: backward_kernel(fold, T, D, FF, r, rd, refs),
        name="backward",
        out_shape=[shape((rows, Q, D)), shape((rows, Q, D)), shape((4, r, D), F32), shape((r, FF), F32), shape((rd, D), F32),
                   shape((VROWS, 128), F32)],
        in_specs=[vm_spec, vm_spec] + [any_spec] * len(saved),
        out_specs=[any_spec, any_spec, vm_spec, vm_spec, vm_spec, vm_spec],
        scratch_shapes=[
            VMEM((4, D, D), BF), VMEM((D, FF), BF), VMEM((T, D), BF), VMEM((3, T, D), BF), VMEM((T, D), BF),
            VMEM((6, 8, T), F32), VMEM((T, D), BF), VMEM((T, D), F32), VMEM((T, 128), F32), VMEM((T, FF), BF),
            VMEM((T, FF), BF), VMEM((T, D), F32), VMEM((T, D), BF), VMEM((VROWS, D), F32), VMEM((VROWS, D), F32),
            VMEM((T, D), BF), VMEM((T, D), BF), VMEM((3, T, D), BF),
        ] + [VMEM((2, 2) + parts[i][:2], BF) for i in (0, 1, 3, 5, 6)]
        + bufs(lambda n, w, line: (2, 2, n, w)) + bufs(lambda n, w, line: (2, 2, n, w))
        + bufs(lambda n, w, line: (2, 2, n // 2, w)) + bufs(lambda n, w, line: (2, n // 2, w))
        + bufs(lambda n, w, line: (4, n // 4, w)) + bufs(lambda n, w, line: (5 if line else 3, n // 4, w)) + [
            VMEM((4, VROWS, D), F32), VMEM((6, VROWS, D), F32),
        ] + sems,
        compiler_params=pltpu.CompilerParams(collective_id=1, has_side_effects=True, vmem_limit_bytes=61 * 2**20),
    )
    reduced = bwd(segment_ids, pad_mask, *kept)

    def line_of(n):
        return shape((1, n), F32)

    done = pl.pallas_call(
        finish_kernel,
        name="finish",
        out_shape=[shape((rows, Q, D)), shape((rows, Q, D))] + [shape((r, D), F32)] * 4 + [shape((r, FF), F32), shape((rd, D), F32)]
        + [line_of(r)] * 5 + [line_of(4 * r)] + [line_of(r)] * 3,
        in_specs=[any_spec] * 5 + [vm_spec],
        out_specs=[any_spec] * 8 + [vm_spec] * 9,
        scratch_shapes=[VMEM((rows, Q, D), BF), VMEM((rows, Q, D), BF), VMEM((4, r, D), F32), VMEM((r, FF), F32), VMEM((rd, D), F32),
                        pltpu.SemaphoreType.DMA((13,))],
        compiler_params=pltpu.CompilerParams(vmem_limit_bytes=60 * 2**20),
    )(*reduced)
    block_out, grad_in, gq, gk, gvv, go, gu, gd = done[:8]
    bq, bv, bo, ga, sa, bu, bd, gf, sf = [v.reshape(-1) for v in done[8:]]
    grads = [gq, bq, gk, gvv, bv, go, bo, ga, sa, gu, bu, gd, bd, gf, sf]
    if fold > 1:
        def narrow(g):
            n = g.shape[0]
            whole = jnp.zeros((32 * n,) + g.shape[1:], F32)
            whole = lax.dynamic_update_slice_in_dim(whole, g, part * n, 0)
            return lax.psum_scatter(whole, ("batch", "seq"), scatter_dimension=0, tiled=True)
        grads = [narrow(g) for g in grads]
    return (block_out, grad_in) + tuple(grads)


def solution(mesh):
    fold = mesh.shape["batch"] // 8
    mat, vec = P(("batch", "seq"), None), P(("batch", "seq"))
    act, rows = P("batch", "seq", None), P("batch", None)
    kinds = [mat, vec, mat, mat, vec, mat, vec, vec, vec, mat, vec, mat, vec, vec, vec]
    return jax.shard_map(
        lambda *args: per_device(fold, *args),
        mesh=mesh,
        in_specs=tuple([act, rows, rows, act] + kinds),
        out_specs=tuple([act, act] + kinds),
        check_vma=False,
    )
```

```python
import jax
import jax.numpy as jnp
from jax import lax
from jax.experimental import pallas as pl
from jax.experimental.pallas import tpu as pltpu
from jax.sharding import PartitionSpec as P

BF = jnp.bfloat16
F32 = jnp.float32
MESH = pl.DeviceIdType.MESH
EPS = 1e-5
NEG = -1e9
C0 = 0.7978845608028654
C1 = 0.044715
NN = (((1,), (0,)), ((), ()))
NT = (((1,), (1,)), ((), ()))
TN = (((0,), (0,)), ((), ()))
VMEM = pltpu.VMEM
ANY = pl.ANY
ROW_BQ, ROW_BV, ROW_BO, ROW_GA, ROW_SA, ROW_BD, ROW_GF, ROW_SF, ROW_UP = 0, 2, 3, 4, 5, 6, 7, 8, 9
VROWS = 16


def dg(a, b, dims):
    return lax.dot_general(a, b, dims, preferred_element_type=F32)


def ds(start, size):
    return pl.ds(pl.multiple_of(start, size), size)


class Place:
    def __init__(self, fold):
        bidx = lax.axis_index("batch")
        z = lax.axis_index("seq")
        hi = bidx // fold
        lo = bidx % fold
        y = hi // 4
        x = (hi // 2) % 2
        c = hi % 2
        self.y, self.x, self.c, self.z, self.b = y, x, c, z, hi
        self.k = hi * 4 + z
        self.bx = y * 4 + (1 - x) * 2 + c
        self.by = (1 - y) * 4 + x * 2 + c
        self.bd = (1 - y) * 4 + (1 - x) * 2 + c
        self.bc = y * 4 + x * 2 + (1 - c)

        def dev(block):
            return (block * fold + lo, z)

        self.xdev, self.ydev, self.cdev = dev(self.bx), dev(self.by), dev(self.bc)
        self.zidx = [z + 1 - 2 * (z % 2), z + 2 - 4 * (z // 2), 3 - z]
        self.zfrom = self.zidx
        self.zdev = [(bidx, zi) for zi in self.zidx]
        self.zp = z + 1 - 2 * (z % 2)
        self.inner = (z == 1) | (z == 2)
        self.outer = (z == 0) | (z == 3)
        self.zm = 3 - z
        self.pdev, self.mdev = (bidx, self.zp), (bidx, self.zm)

    def greet(self):
        bar = pltpu.get_barrier_semaphore()
        for d in [self.xdev, self.ydev, self.cdev] + self.zdev:
            pl.semaphore_signal(bar, inc=1, device_id=d, device_id_type=MESH)
        pl.semaphore_wait(bar, 6)


class Wire:
    def __init__(self, send_sems, recv_sems):
        self.ss, self.rs, self.n, self.open, self.cond = send_sems, recv_sems, 0, [], None

    def when(self, cond, body):
        @pl.when(cond)
        def _():
            self.cond = cond
            body()
            self.cond = None

    def send(self, src, dst, device):
        i = self.n
        self.n += 1

        def make():
            return pltpu.make_async_remote_copy(src_ref=src(), dst_ref=dst(), send_sem=self.ss.at[i], recv_sem=self.rs.at[i],
                                                device_id=device, device_id_type=MESH)

        make().start()
        tag = (i, device, make, self.cond)
        self.open.append(tag)
        return tag

    def recv(self, tag, dst):
        i, device = tag[:2]
        pltpu.make_async_remote_copy(src_ref=dst, dst_ref=dst, send_sem=self.ss.at[i], recv_sem=self.rs.at[i],
                                     device_id=device, device_id_type=MESH).wait_recv()

    def sent(self, tag):
        tag[2]().wait_send()
        self.open = [other for other in self.open if other is not tag]

    def finish(self):
        for tag in self.open:
            if tag[3] is None:
                tag[2]().wait_send()
            else:
                pl.when(tag[3])(lambda tag=tag: tag[2]().wait_send())
        self.open = []


class Local:
    def __init__(self, sems):
        self.sems, self.n, self.open = sems, 0, []

    def start(self, src, dst):
        i = self.n
        self.n += 1

        def make():
            return pltpu.make_async_copy(src(), dst(), self.sems.at[i])

        make().start()
        self.open.append(make)
        return make

    def wait(self, make):
        make().wait()
        self.open = [other for other in self.open if other is not make]

    def finish(self):
        for make in self.open:
            make().wait()
        self.open = []


def norm_rows(v, gain, shift):
    center = v - jnp.mean(v, axis=-1, keepdims=True)
    inv = lax.rsqrt(jnp.mean(center * center, axis=-1, keepdims=True) + EPS)
    xhat = center * inv
    return xhat * gain + shift, xhat, inv


def norm_back(g, xhat, inv, gain):
    e = g * gain
    return inv * (e - jnp.mean(e, axis=-1, keepdims=True) - xhat * jnp.mean(e * xhat, axis=-1, keepdims=True))


def rows_sum(v):
    return jnp.sum(v, axis=0, keepdims=True)


def place_matrix(rows, width, start, count):
    i = lax.broadcasted_iota(jnp.int32, (rows, width), 0)
    j = lax.broadcasted_iota(jnp.int32, (rows, width), 1)
    return jnp.where((j == start + i) & (i < count), 1.0, 0.0).astype(BF)


def segments(seg_ref, pad_ref, z, length):
    seg = seg_ref[pl.ds(z, 1), :].astype(F32)
    live = pad_ref[pl.ds(z, 1), :]
    keyed = jnp.where(live == 1, seg, -1.0)

    def column(row):
        return jnp.broadcast_to(row, (128, length)).T[:, 0:1]

    return seg, keyed, column


def forward_kernel(fold, T, D, FF, r, rd,
                   hidden, cot, seg, pad, wq, wk, wv, wo, wu, wd,
                   v0, v1, v2, v3, v4, v5, v6, v7, v8,
                   o_tok, o_qkv, o_att, o_lse, o_nlow, o_xh1, o_inv1, o_act, o_gp, o_gmid, o_gffn, o_out, o_vec,
                   o_gvec, o_wA, o_wU, o_wD,
                   zA, zU, wA, wU, wD, tok, cotr, qkv, att, lse, nlow, xh1, inv1, normed, act, gp, tmp, gffn, out,
                   vec, gvec, table, vsend, vland, ss, rs, ls):
    me = Place(fold)
    wire = Wire(ss, rs)
    local = Local(ls)
    z, b = me.z, me.b
    Q = T // 4
    block, dblock = 4 * r, 4 * rd

    def drow(k, sub):
        return wD.at[k // 2, ds((k % 2) * dblock + sub * rd, rd)]

    def dhalf(k, sub, cols):
        return wD.at[k // 2, ds((k % 2) * dblock + sub * rd, rd), cols]

    own = [local.start(lambda w=w: w, lambda i=i: zA.at[i, z]) for i, w in enumerate((wq, wk, wv, wo))]
    own_u = local.start(lambda: wu, lambda: zU.at[z])
    own_d = local.start(lambda: wd, lambda: drow(b, z))
    own_t = local.start(lambda: hidden.at[z], lambda: tok.at[ds(z * Q, Q)])
    own_c = local.start(lambda: cot.at[z], lambda: cotr.at[ds(z * Q, Q)])

    table[...] = jnp.zeros_like(table)
    for i, ref in zip((ROW_BQ, ROW_BV, ROW_BO, ROW_GA, ROW_SA, ROW_BD, ROW_GF, ROW_SF, ROW_UP), (v0, v1, v2, v3, v4, v5, v6, v7, v8)):
        table[i:i + 1, 0:ref.shape[1]] = ref[...].astype(F32)
    given = table[...].astype(BF)
    v_a = dg(given, place_matrix(128, D, me.k * r, r), NN)
    per_row = D // block
    v_u = dg(given, place_matrix(128, D, (me.k % per_row) * block, block), NN)[ROW_UP:ROW_UP + 1]
    ri = lax.broadcasted_iota(jnp.int32, (VROWS, D), 0)
    up_row = ROW_UP + me.k // per_row
    vsend[0] = jnp.where(ri < ROW_UP, v_a, jnp.where(ri == up_row, jnp.broadcast_to(v_u, (VROWS, D)), 0.0)).astype(BF)

    me.greet()

    def zsend(src, dst):
        return [wire.send(lambda k=k: src(k), dst, me.zdev[k]) for k in range(3)]

    def zrecv(tags, dst):
        for k in range(3):
            wire.recv(tags[k], dst(k))

    class Spread:
        def __init__(self, region):
            self.region = region

        def go(self, k, half, n, device):
            return wire.send(lambda: self.region(k, half, n), lambda: self.region(k, half, n), device)

        def own(self):
            self.tx = self.go(b, 0, 2, me.xdev)
            self.ty = self.go(b, 0, 2, me.ydev)
            self.tc = [self.go(b, 0, 2, me.cdev)]

        def mid(self):
            g = self.region
            wire.recv(self.tx, g(me.bx, 0, 2))
            self.f1 = self.go(me.bx, 0, 1, me.ydev)
            wire.recv(self.ty, g(me.by, 0, 2))
            self.f2 = self.go(me.by, 1, 1, me.xdev)
            self.tc.append(self.go(me.bx, 0, 2, me.cdev))
            self.tc.append(self.go(me.by, 0, 2, me.cdev))

        def last(self):
            g = self.region
            wire.recv(self.f1, g(me.bd, 0, 1))
            wire.recv(self.f2, g(me.bd, 1, 1))
            self.tc.append(self.go(me.bd, 0, 2, me.cdev))

        def done(self):
            for tag, k in zip(self.tc, (me.b, me.bx, me.by, me.bd)):
                wire.recv(tag, self.region(k + 1 - 2 * me.c, 0, 2))

    def part(k, half, n, size):
        h = size // 2
        return ds(k * size + half * h, h) if n == 1 else ds(k * size, size)

    hF, hD = FF // 2, D // 2
    s_qkv = Spread(lambda k, half, n: wA.at[0:3, part(k, half, n, block)])
    s_o = Spread(lambda k, half, n: wA.at[3, part(k, half, n, block)])
    s_u = [Spread(lambda k, half, n, i=i: wU.at[part(k, half, n, block), i * hF:(i + 1) * hF]) for i in range(2)]
    s_d = [Spread(lambda k, half, n, i=i: wD.at[k // 2, part(k % 2, half, n, dblock), i * hD:(i + 1) * hD]) for i in range(2)]


    def join(parts):
        return jnp.concatenate([p.astype(F32) for p in parts], axis=0).astype(BF)

    t_vec = [wire.send(lambda: vsend.at[0], lambda k=k: vland.at[k], me.zdev[k]) for k in range(3)]
    for cp in own[:3]:
        local.wait(cp)
    t_qkv = zsend(lambda k: zA.at[0:3, z], lambda: zA.at[0:3, z])
    t_u = zsend(lambda k: wu, lambda: zU.at[z])
    t_hid = zsend(lambda k: hidden.at[me.zidx[k]], lambda: tok.at[ds(z * Q, Q)])
    local.wait(own[3])
    t_o = zsend(lambda k: zA.at[3, z], lambda: zA.at[3, z])
    halves = [slice(0, hD), slice(hD, D)]
    t_d = [zsend(lambda k, h=h: wd.at[:, h], lambda h=h: dhalf(b, z, h)) for h in halves]

    zrecv(t_vec, lambda k: vland.at[k])
    vsend[1] = vsend[0] + vland[0] + vland[1] + vland[2]
    tv = wire.send(lambda: vsend.at[1], lambda: vland.at[3], me.xdev)

    zrecv(t_qkv, lambda k: zA.at[0:3, me.zfrom[k]])
    for i in range(3):
        wA[i, ds(b * block, block), :] = join([zA[i, s] for s in range(4)])
    s_qkv.own()
    wire.recv(tv, vland.at[3])
    vsend[2] = vsend[1] + vland[3]
    tv = wire.send(lambda: vsend.at[2], lambda: vland.at[4], me.ydev)
    s_qkv.mid()
    wire.recv(tv, vland.at[4])
    vsend[3] = vsend[2] + vland[4]
    tv = wire.send(lambda: vsend.at[3], lambda: vland.at[5], me.cdev)
    local.wait(own_u)
    zrecv(t_u, lambda k: zU.at[me.zfrom[k]])
    wU[ds(b * block, block), :] = join([zU[s] for s in range(4)])
    s_u[0].own()
    s_u[1].own()
    s_qkv.last()
    wire.recv(tv, vland.at[5])
    vec[...] = vsend[3].astype(F32) + vland[5].astype(F32)
    local.start(lambda: vec, lambda: o_vec)
    s_qkv.done()
    s_u[0].mid()
    local.wait(own_t)
    zrecv(t_hid, lambda k: tok.at[ds(me.zfrom[k] * Q, Q)])
    local.start(lambda: tok, lambda: o_tok)

    def project(j):
        v = dg(tok[...], wA[j], NN) + vec[pl.ds(j, 1), :]
        v = v.astype(BF)
        qkv[j] = v * jnp.where(j == 0, 0.125, 1.0).astype(BF)

    pl.loop(0, 3)(project)
    local.start(lambda: qkv, lambda: o_qkv)
    s_u[1].mid()
    zrecv(t_o, lambda k: zA.at[3, me.zfrom[k]])
    wA[3, ds(b * block, block), :] = join([zA[3, s] for s in range(4)])
    s_o.own()

    seg_row, key_row, column = segments(seg, pad, z, T)
    seg_col = column(seg_row)
    lane = lax.broadcasted_iota(jnp.int32, (T, 128), 1)
    lo = lane < 64

    def attend(p):
        o = ds(p * 128, 128)
        k = qkv[1, :, o]
        v = qkv[2, :, o]
        one = jnp.ones_like(v)
        zero = jnp.zeros_like(v)
        v0_, v1_ = jnp.where(lo, v, one), jnp.where(lo, one, v)
        k0, k1 = jnp.where(lo, k, zero), jnp.where(lo, zero, k)
        q = qkv[0, :, o]
        ok = seg_col == key_row
        res, top = [], []
        for kk, vv in ((k0, v0_), (k1, v1_)):
            s = jnp.where(ok, dg(q, kk, NT), NEG)
            m = jnp.max(s, axis=-1, keepdims=True)
            res.append(dg(jnp.exp(s - m).astype(BF), vv, NN))
            top.append(m)
        num = jnp.where(lo, res[0], res[1])
        den = pltpu.roll(jnp.where(lo, res[1], res[0]), 64, 1)
        att[:, o] = (num / den).astype(BF)
        lt = (jnp.log(den) + jnp.where(lo, top[0], top[1])).T
        lse[p, 0:1, :] = lt[0:1]
        lse[p, 1:2, :] = lt[64:65]

    tags = {}

    def serve0():
        s_u[0].last()

    def serve1():
        pass

    def serve2():
        local.wait(own_d)
        zrecv(t_d[0], lambda k: dhalf(b, me.zfrom[k], halves[0]))
        s_d[0].own()
        s_o.mid()

    def serve3():
        s_u[1].last()

    def serve4():
        zrecv(t_d[1], lambda k: dhalf(b, me.zfrom[k], halves[1]))
        s_d[1].own()
        tags["cot"] = zsend(lambda k: cot.at[me.zidx[k]], lambda: cotr.at[ds(z * Q, Q)])
        s_o.last()

    def serve5():
        s_d[0].mid()

    services = [serve0, serve1, serve2, serve3, serve4, serve5]

    @pl.loop(0, 6)
    def _(p):
        attend(p)
        for i, service in enumerate(services):
            pl.when(p == i)(service)

    local.start(lambda: att, lambda: o_att)
    local.start(lambda: lse, lambda: o_lse)
    s_o.done()
    local.start(lambda: wA, lambda: o_wA)
    tmp[...] = dg(att[...], wA[3], NN) + vec[ROW_BO:ROW_BO + 1, :]

    def norm_one(i):
        rr = ds(i * 64, 64)
        y_, xh, inv = norm_rows(tmp[rr, :] + tok[rr, :].astype(F32), vec[ROW_GA:ROW_GA + 1, :], vec[ROW_SA:ROW_SA + 1, :])
        normed[rr, :] = y_
        nlow[rr, :] = y_.astype(BF)
        xh1[rr, :] = xh
        inv1[rr, :] = jnp.broadcast_to(inv, (64, 128))

    pl.loop(0, T // 64)(norm_one)
    local.start(lambda: nlow, lambda: o_nlow)
    local.start(lambda: xh1, lambda: o_xh1)
    local.start(lambda: inv1, lambda: o_inv1)
    s_u[0].done()
    s_u[1].done()
    local.start(lambda: wU, lambda: o_wU)

    wide = D // 2

    def up(j):
        o = ds(j * wide, wide)
        bias = vec[pl.ds(ROW_UP + j // 2, 1), ds((j % 2) * wide, wide)]
        v = dg(nlow[...], wU[:, o], NN) + bias
        v2 = v * v
        t = jnp.tanh(v * (C0 + C0 * C1 * v2))
        half = 0.5 * (1 + t)
        act[:, o] = (v * half).astype(BF)
        gp[:, o] = (half + 0.5 * v * (1 - t * t) * (C0 + 3 * C0 * C1 * v2)).astype(BF)

    @pl.loop(0, FF // wide)
    def _(j):
        up(j)
        pl.when(j == 2)(s_d[1].mid)

    local.start(lambda: act, lambda: o_act)
    local.start(lambda: gp, lambda: o_gp)
    s_d[0].last()
    s_d[1].last()
    s_d[0].done()
    s_d[1].done()
    local.start(lambda: wD, lambda: o_wD)

    tmp[...] = dg(act[:, 0:D], wD[0], NN) + vec[ROW_BD:ROW_BD + 1, :]

    def down(j):
        tmp[...] += dg(act[:, ds(j * D, D)], wD[j], NN)

    pl.loop(1, FF // D)(down)
    local.wait(own_c)
    zrecv(tags["cot"], lambda k: cotr.at[ds(me.zfrom[k] * Q, Q)])
    zero_row = jnp.zeros((1, D), F32)
    gvec[...] = jnp.zeros_like(gvec)

    def norm_two(i, sums):
        rr = ds(i * 64, 64)
        gain = vec[ROW_GF:ROW_GF + 1, :]
        y_, xh, inv = norm_rows(tmp[rr, :] + normed[rr, :], gain, vec[ROW_SF:ROW_SF + 1, :])
        out[rr, :] = y_.astype(BF)
        g = cotr[rr, :].astype(F32)
        gm = norm_back(g, xh, inv, gain)
        gl = gm.astype(BF)
        tmp[rr, :] = gm
        gffn[rr, :] = gl
        return sums[0] + rows_sum(g * xh), sums[1] + rows_sum(g), sums[2] + rows_sum(gl.astype(F32))

    s0, s1, s2 = lax.fori_loop(0, T // 64, norm_two, (zero_row, zero_row, zero_row))
    gvec[ROW_GF:ROW_GF + 1, :] = s0
    gvec[ROW_SF:ROW_SF + 1, :] = s1
    gvec[ROW_BD:ROW_BD + 1, :] = s2
    local.start(lambda: gffn, lambda: o_gffn)
    local.start(lambda: out, lambda: o_out)
    local.start(lambda: tmp, lambda: o_gmid)
    local.start(lambda: gvec, lambda: o_gvec)
    wire.finish()
    local.finish()


def backward_kernel(fold, T, D, FF, r, rd, refs):
    take = iter(refs)

    def some(n):
        return [next(take) for _ in range(n)]

    (seg, pad, i_tok, i_qkv, i_att, i_lse, i_nlow, i_xh1, i_inv1, i_act, i_gp, i_gmid, i_gffn, i_out,
     i_vec, i_gvec, i_wA, i_wU, i_wD) = some(19)
    bout, gin_out, gA_out, gU_out, gD_out, gv_out = some(6)
    (w1, wU, tok, qkv, att, lse, nlow, xh1, inv1, act, gp, gmid, gffn, vec, gvec, gattn, gatt, gqkv) = some(18)
    d_snd0, d_snd1, u_snd, o_snd, a_snd = some(5)
    mines, ones, firsts, seconds, outs, ins = [some(8) for _ in range(6)]
    vsend, vland, ss, rs, ls = some(5)

    me = Place(fold)
    wire = Wire(ss, rs)
    local = Local(ls)
    z, b, c, x, y = me.z, me.b, me.c, me.x, me.y
    Q = T // 4

    def load(src, dst):
        return local.start(lambda: src, lambda: dst)

    l_act, l_gffn = load(i_act, act), load(i_gffn, gffn)
    me.greet()
    t_out = [wire.send(lambda k=k: i_out.at[ds(me.zidx[k] * Q, Q)], lambda: bout.at[z], me.zdev[k]) for k in range(3)]

    def keep(v0, v1):
        first = c == 0
        return jnp.where(first, v0, v1).astype(BF), jnp.where(first, v1, v0).astype(BF)

    def plus(a, e):
        return (a.astype(F32) + e.astype(F32)).astype(BF)

    class Sum:
        def __init__(self, i, snd, rows, line, write):
            self.snd, self.rows, self.line, self.write = snd, rows, line, write
            self.mine, self.r1, self.ra, self.rb, self.zs, self.zr = (mines[i], ones[i], firsts[i], seconds[i], outs[i], ins[i])

        def core(self):
            self.tc = wire.send(lambda: self.snd, lambda: self.r1, me.cdev)

        def plane_one(self):
            n = 2 * self.rows
            wire.recv(self.tc, self.r1)

            @pl.loop(0, 2)
            def _(i):
                for j in range(2):
                    self.mine[i, j] = plus(self.mine[i, j], self.r1[i, j])

            self.tx = wire.send(lambda: self.mine.at[:, 1 - x, 0:n], lambda: self.ra.at[0], me.xdev)
            self.ty = wire.send(lambda: self.mine.at[1 - y, :, n:2 * n], lambda: self.ra.at[1], me.ydev)

        def plane_two(self):
            n = 2 * self.rows
            wire.recv(self.tx, self.ra.at[0])
            for i in range(2):
                self.mine[i, x, 0:n] = plus(self.mine[i, x, 0:n], self.ra[0, i])
            self.ty2 = wire.send(lambda: self.mine.at[1 - y, x, 0:n], lambda: self.rb.at[0], me.ydev)
            wire.recv(self.ty, self.ra.at[1])
            for i in range(2):
                self.mine[y, i, n:2 * n] = plus(self.mine[y, i, n:2 * n], self.ra[1, i])
            self.tx2 = wire.send(lambda: self.mine.at[y, 1 - x, n:2 * n], lambda: self.rb.at[1], me.xdev)

        def along(self):
            n = 2 * self.rows
            q = self.rows
            for half, tag in ((0, self.ty2), (1, self.tx2)):
                wire.recv(tag, self.rb.at[half])
                v = self.mine[y, x, half * n:(half + 1) * n].astype(F32) + self.rb[half].astype(F32)
                self.zs[2 * half] = v[0:q].astype(BF)
                self.zs[2 * half + 1] = v[q:2 * q].astype(BF)
            if self.line:
                def outer():
                    self.t1 = wire.send(lambda: self.zs.at[pl.ds(jnp.where(z == 0, 1, 0), 3)], lambda: self.zr.at[0:3], me.pdev)

                wire.when(me.outer, outer)
            else:
                self.tz = [wire.send(lambda k=k: self.zs.at[me.zidx[k]], lambda k=k: self.zr.at[k], me.zdev[k]) for k in range(3)]

        def line_one(self):
            def inner():
                wire.recv(self.t1, self.zr.at[0:3])
                base = jnp.where(z == 1, 1, 0)
                start = jnp.where(z == 1, 2, 0)
                for i in range(2):
                    self.zs[start + i] = plus(self.zs[start + i], self.zr[start + i - base])
                self.t2 = wire.send(lambda: self.zs.at[pl.ds(jnp.where(z == 1, 2, 0), 2)], lambda: self.zr.at[3:5], me.mdev)

            wire.when(me.inner, inner)

        def line_two(self):
            def inner():
                wire.recv(self.t2, self.zr.at[3:5])
                base = jnp.where(z == 1, 1, 0)
                pair = jnp.where(z == 1, 0, 2)
                self.zs[me.zp] = plus(self.zs[me.zp], self.zr[3 + me.zp - pair])
                self.t3 = wire.send(lambda: self.zs.at[me.zp], lambda: self.zr.at[0], me.pdev)
                self.write(self.zs[z].astype(F32) + self.zr[z - base].astype(F32) + self.zr[3 + z - pair].astype(F32))

            wire.when(me.inner, inner)

        def done(self):
            if self.line:
                def outer():
                    wire.recv(self.t3, self.zr.at[0])
                    self.write(self.zs[z].astype(F32) + self.zr[0].astype(F32))

                wire.when(me.outer, outer)
            else:
                v = self.zs[z].astype(F32)
                for k in range(3):
                    wire.recv(self.tz[k], self.zr.at[k])
                    v = v + self.zr[k].astype(F32)
                self.write(v)

    third, hF, hD = D // 3, FF // 2, D // 2

    def write_d(i):
        def f(v):
            gD_out[:, i * third:(i + 1) * third] = v
        return f

    def write_u(i):
        def f(v):
            gU_out[:, i * hF:(i + 1) * hF] = v
        return f

    def write_o(v):
        gA_out[3] = v

    def write_a(i):
        def f(v):
            for m in range(3):
                gA_out[m, :, i * hD:(i + 1) * hD] = v[:, m * hD:(m + 1) * hD]
        return f

    D0 = Sum(0, d_snd0, rd, False, write_d(0))
    D1 = Sum(1, d_snd1, rd, False, write_d(1))
    D2 = Sum(2, d_snd0, rd, False, write_d(2))
    U0 = Sum(3, u_snd, r, False, write_u(0))
    U1 = Sum(4, u_snd, r, True, write_u(1))
    O = Sum(5, o_snd, r, False, write_o)
    A0 = Sum(6, a_snd, r, False, write_a(0))
    A1 = Sum(7, a_snd, r, False, write_a(1))

    def down_grad(part, i):
        cols = slice(i * third, (i + 1) * third)

        @pl.loop(0, 4)
        def _(i):
            v = dg(act[:, ds(i * D, D)], gffn[:, cols], TN)
            mine, theirs = keep(v[0:4 * rd], v[4 * rd:8 * rd])
            part.mine[i // 2, i % 2] = mine
            part.snd[i // 2, i % 2] = theirs

    def store(part, v, cols):
        n = 4 * r
        for i in range(4):
            mine, theirs = keep(v[(2 * i) * n:(2 * i + 1) * n], v[(2 * i + 1) * n:(2 * i + 2) * n])
            part.mine[i // 2, i % 2, :, cols] = mine
            part.snd[i // 2, i % 2, :, cols] = theirs

    def inner(j):
        o = ds(j * D, D)
        gi = (dg(gffn[...], w1[j], NT) * gp[:, o].astype(F32)).astype(BF)
        gp[:, o] = gi
        gvec[pl.ds(ROW_UP + j, 1), :] = rows_sum(gi.astype(F32))

    def up_grad(part, first):
        wide = hF // 3

        @pl.loop(0, 3)
        def _(j):
            o = ds(j * wide, wide)
            store(part, dg(nlow[...], gp[:, ds(first + j * wide, wide)], TN), o)

    local.wait(l_act)
    local.wait(l_gffn)
    l_wD, l_gp = load(i_wD, w1), load(i_gp, gp)
    down_grad(D0, 0)
    D0.core()
    l_gvec, l_nlow, l_gmid, l_wU = load(i_gvec, gvec), load(i_nlow, nlow), load(i_gmid, gmid), load(i_wU, wU)
    down_grad(D1, 1)
    D1.core()
    l_vec, l_xh1, l_inv1, l_att = load(i_vec, vec), load(i_xh1, xh1), load(i_inv1, inv1), load(i_att, att)
    l_qkv, l_lse, l_tok = load(i_qkv, qkv), load(i_lse, lse), load(i_tok, tok)
    local.start(lambda: i_out.at[ds(z * Q, Q)], lambda: bout.at[z])
    D0.plane_one()
    wire.sent(D0.tc)
    down_grad(D2, 2)
    D2.core()
    D1.plane_one()
    local.wait(l_wD)
    local.wait(l_gp)
    local.wait(l_gvec)
    pl.loop(0, FF // D)(inner)
    l_wA = load(i_wA, w1)
    D0.plane_two()
    D2.plane_one()
    local.wait(l_wU)
    local.wait(l_gmid)
    gmid[...] += dg(gp[...], wU[...], NT)
    local.wait(l_vec)
    local.wait(l_xh1)
    local.wait(l_inv1)
    zero_row = jnp.zeros((1, D), F32)

    def norm_one(i, sums):
        rr = ds(i * 64, 64)
        g = gmid[rr, :]
        xh = xh1[rr, :]
        gm = norm_back(g, xh, inv1[rr, 0:1], vec[ROW_GA:ROW_GA + 1, :])
        gl = gm.astype(BF)
        gmid[rr, :] = gm
        gattn[rr, :] = gl
        return sums[0] + rows_sum(g * xh), sums[1] + rows_sum(g), sums[2] + rows_sum(gl.astype(F32))

    s0, s1, s2 = lax.fori_loop(0, T // 64, norm_one, (zero_row, zero_row, zero_row))
    gvec[ROW_GA:ROW_GA + 1, :] = s0
    gvec[ROW_SA:ROW_SA + 1, :] = s1
    gvec[ROW_BO:ROW_BO + 1, :] = s2
    D1.plane_two()
    local.wait(l_nlow)
    up_grad(U0, 0)
    U0.core()
    local.wait(l_att)
    local.wait(l_wA)
    gatt[...] = dg(gattn[...], w1[3], NT).astype(BF)
    local.wait(l_qkv)
    local.wait(l_lse)
    local.wait(l_tok)

    seg_row, key_row, column = segments(seg, pad, z, T)
    key_col = column(key_row)
    lane = lax.broadcasted_iota(jnp.int32, (T, 128), 1)
    lo = lane < 64
    pick = (lax.broadcasted_iota(jnp.int32, (8, 128), 1) // 64 == lax.broadcasted_iota(jnp.int32, (8, 128), 0)).astype(BF)

    def attend(p):
        o = ds(p * 128, 128)
        q = qkv[0, :, o]
        k = qkv[1, :, o]
        g = gatt[:, o]
        prod = g.astype(F32) * att[:, o].astype(F32)
        hi = prod.astype(BF)
        rest = (prod - hi.astype(F32)).astype(BF)
        delta = dg(pick, hi, NT) + dg(pick, rest, NT)
        zero = jnp.zeros_like(q)
        qm = (jnp.where(lo, q, zero), jnp.where(lo, zero, q))
        gm = (jnp.where(lo, g, zero), jnp.where(lo, zero, g))
        km = (jnp.where(lo, k, zero), jnp.where(lo, zero, k))
        dq = jnp.zeros((T, 128), F32)
        half = T // 2
        for step in range(2):
            rows = slice(step * half, (step + 1) * half)
            kc = qkv[1, rows, o]
            vc = qkv[2, rows, o]
            ok = key_col[rows] == seg_row
            dk = jnp.zeros((half, 128), F32)
            dv = jnp.zeros((half, 128), F32)
            for hh in range(2):
                s = jnp.where(ok, dg(kc, qm[hh], NT), NEG)
                pt = jnp.exp(s - lse[p, hh:hh + 1, :])
                dp = dg(vc, gm[hh], NT)
                dsc = (pt * (dp - delta[hh:hh + 1, :])).astype(BF)
                dv = dv + dg(pt.astype(BF), gm[hh], NN)
                dk = dk + dg(dsc, qm[hh], NN)
                dq = dq + dg(dsc, km[hh][rows], TN)
            gqkv[1, rows, o] = dk.astype(BF)
            gqkv[2, rows, o] = dv.astype(BF)
        gqkv[0, :, o] = (dq * 0.125).astype(BF)

    def qkv_grad(part, first):
        @pl.loop(0, 3)
        def _(j):
            store(part, dg(tok[...], gqkv[j, :, first:first + hD], TN), ds(j * hD, hD))

    def serve0():
        U0.plane_one()
        D2.plane_two()
        D0.along()

    def serve1():
        D1.along()
        wire.sent(U0.tc)
        up_grad(U1, hF)
        U1.core()

    def serve2():
        U1.plane_one()
        D0.done()

    def serve3():
        U0.plane_two()

    def serve4():
        D1.done()
        D2.along()

    def serve5():
        pass

    services = [serve0, serve1, serve2, serve3, serve4, serve5]

    @pl.loop(0, 6)
    def _(p):
        attend(p)
        for i, service in enumerate(services):
            pl.when(p == i)(service)

    gin = gatt
    gmid[...] += dg(gqkv[0], w1[0], NT)
    gmid[...] += dg(gqkv[1], w1[1], NT)
    gin[...] = (gmid[...] + dg(gqkv[2], w1[2], NT)).astype(BF)
    local.start(lambda: gin.at[ds(z * Q, Q)], lambda: gin_out.at[z])
    t_gin = [wire.send(lambda k=k: gin.at[ds(me.zidx[k] * Q, Q)], lambda: gin_out.at[z], me.zdev[k]) for k in range(3)]
    U1.plane_two()
    grad_o = dg(att[...], gattn[...], TN)
    store(O, grad_o, slice(0, D))
    O.core()
    U0.along()
    O.plane_one()
    qkv_grad(A0, 0)
    A0.core()
    for j, row in ((0, ROW_BQ), (2, ROW_BV)):
        gvec[row:row + 1, :] = rows_sum(gqkv[j].astype(F32))
    tv = wire.send(lambda: gvec, lambda: vland.at[0], me.cdev)
    A0.plane_one()
    wire.sent(A0.tc)
    qkv_grad(A1, hD)
    A1.core()
    D2.done()
    wire.recv(tv, vland.at[0])
    vsend[0] = gvec[...] + vland[0]
    tv = wire.send(lambda: vsend.at[0], lambda: vland.at[1], me.xdev)
    O.plane_two()
    U1.along()
    A1.plane_one()
    wire.recv(tv, vland.at[1])
    vsend[1] = vsend[0] + vland[1]
    tv = wire.send(lambda: vsend.at[1], lambda: vland.at[2], me.ydev)
    A0.plane_two()
    O.along()
    wire.recv(tv, vland.at[2])
    vsend[2] = vsend[1] + vland[2]
    tvs = [wire.send(lambda: vsend.at[2], lambda k=k: vland.at[3 + k], me.zdev[k]) for k in range(3)]
    A1.plane_two()
    U1.line_one()
    A0.along()
    A1.along()
    U0.done()
    U1.line_two()
    U1.done()
    O.done()
    total = vsend[2]
    for k in range(3):
        wire.recv(tvs[k], vland.at[3 + k])
        total = total + vland[3 + k]
    vsend[3] = total

    def exact(v, m):
        a = v.astype(BF)
        v = v - a.astype(F32)
        e = v.astype(BF)
        v = (v - e.astype(F32)).astype(BF)
        return dg(a, m, NT) + dg(e, m, NT) + dg(v, m, NT)

    per_row = D // (4 * r)
    gv = exact(total, place_matrix(128, D, me.k * r, r))
    row = vsend[3, pl.ds(ROW_UP + me.k // per_row, 1), :]
    gu = exact(jnp.broadcast_to(row, (VROWS, D)), place_matrix(128, D, (me.k % per_row) * (4 * r), 4 * r))
    ri = lax.broadcasted_iota(jnp.int32, (VROWS, 128), 0)
    gv_out[...] = jnp.where(ri < ROW_UP, gv, gu)
    A0.done()
    A1.done()
    for k in range(3):
        wire.recv(t_out[k], bout.at[me.zfrom[k]])
        wire.recv(t_gin[k], gin_out.at[me.zfrom[k]])
    wire.finish()
    local.finish()


def finish_kernel(bout, gin, gA, gU, gD, gv, o_b, o_g, o_q, o_k, o_v, o_o, o_u, o_d, *rest):
    vecs, (s_b, s_g, s_A, s_U, s_D, sems) = rest[:9], rest[9:]
    loads = [(bout, s_b), (gin, s_g), (gA, s_A), (gU, s_U), (gD, s_D)]
    loads = [pltpu.make_async_copy(src, dst, sems.at[i]) for i, (src, dst) in enumerate(loads)]
    for cp in loads:
        cp.start()
    for row, ref in zip((ROW_BQ, ROW_BV, ROW_BO, ROW_GA, ROW_SA, ROW_UP, ROW_BD, ROW_GF, ROW_SF), vecs):
        ref[...] = gv[row:row + 1, 0:ref.shape[1]]
    stores = [[(s_b, o_b)], [(s_g, o_g)], [(s_A.at[i], ref) for i, ref in enumerate((o_q, o_k, o_v, o_o))], [(s_U, o_u)], [(s_D, o_d)]]
    out, n = [], len(loads)
    for cp, group in zip(loads, stores):
        cp.wait()
        for src, dst in group:
            out.append(pltpu.make_async_copy(src, dst, sems.at[n]))
            out[-1].start()
            n += 1
    for cp in out:
        cp.wait()


def per_device(fold, hidden_in, segment_ids, pad_mask, cotangent, w_query, bias_query, w_key, w_value, bias_value,
               w_out, bias_out, gain_attn, shift_attn, w_up, bias_up, w_down, bias_down, gain_ffn, shift_ffn):
    rows, Q, D = hidden_in.shape
    T = segment_ids.shape[1]
    mats = [w_query, w_key, w_value, w_out, w_up, w_down]
    vecs = [bias_query, bias_value, bias_out, gain_attn, shift_attn, bias_down, gain_ffn, shift_ffn, bias_up]
    hi = lax.axis_index("batch") // fold
    part = hi * 4 + lax.axis_index("seq")
    if fold > 1:
        def widen(w):
            whole = lax.all_gather(w, ("batch", "seq"), axis=0, tiled=True)
            n = w.shape[0] * fold
            return lax.dynamic_slice_in_dim(whole, part * n, n, 0)
        mats = [widen(w) for w in mats]
        vecs = [widen(v) for v in vecs]
    wq, wk, wv, wo, wu, wd = mats
    r, rd, FF = wq.shape[0], wd.shape[0], wu.shape[1]

    def shape(s, d=BF):
        return jax.ShapeDtypeStruct(s, d)

    any_spec = pl.BlockSpec(memory_space=ANY)
    vm_spec = pl.BlockSpec(memory_space=VMEM)
    saved = [shape((T, D)), shape((3, T, D)), shape((T, D)), shape((6, 8, T), F32), shape((T, D)), shape((T, D), F32),
             shape((T, 128), F32), shape((T, FF)), shape((T, FF)), shape((T, D), F32), shape((T, D)), shape((T, D)),
             shape((VROWS, D), F32), shape((VROWS, D), F32), shape((4, D, D)), shape((D, FF)), shape((4, D, D))]
    n_remote = 112
    sems = [pltpu.SemaphoreType.DMA((n_remote,)), pltpu.SemaphoreType.DMA((n_remote,)), pltpu.SemaphoreType.DMA((32,))]
    fwd = pl.pallas_call(
        lambda *refs: forward_kernel(fold, T, D, FF, r, rd, *refs),
        name="forward",
        out_shape=saved,
        in_specs=[any_spec, any_spec, vm_spec, vm_spec] + [any_spec] * 6 + [vm_spec] * 9,
        out_specs=[any_spec] * len(saved),
        scratch_shapes=[
            VMEM((4, 4, r, D), BF), VMEM((4, r, FF), BF), VMEM((4, D, D), BF), VMEM((D, FF), BF), VMEM((4, D, D), BF),
            VMEM((T, D), BF), VMEM((T, D), BF), VMEM((3, T, D), BF), VMEM((T, D), BF), VMEM((6, 8, T), F32),
            VMEM((T, D), BF), VMEM((T, D), F32), VMEM((T, 128), F32), VMEM((T, D), F32), VMEM((T, FF), BF),
            VMEM((T, FF), BF), VMEM((T, D), F32), VMEM((T, D), BF), VMEM((T, D), BF),
            VMEM((VROWS, D), F32), VMEM((VROWS, D), F32), VMEM((VROWS, 128), F32), VMEM((4, VROWS, D), BF),
            VMEM((6, VROWS, D), BF),
        ] + sems,
        compiler_params=pltpu.CompilerParams(collective_id=0, has_side_effects=True, vmem_limit_bytes=58 * 2**20),
    )
    kept = fwd(hidden_in, cotangent, segment_ids, pad_mask, wq, wk, wv, wo, wu, wd, *[v.reshape(1, -1) for v in vecs])

    parts = [(4 * rd, D // 3, False)] * 3 + [(4 * r, FF // 2, False), (4 * r, FF // 2, True)] + [(4 * r, D, False)] + [(4 * r, 3 * D // 2, False)] * 2

    def bufs(f):
        return [VMEM(f(n, w, line), BF) for n, w, line in parts]

    bwd = pl.pallas_call(
        lambda *refs: backward_kernel(fold, T, D, FF, r, rd, refs),
        name="backward",
        out_shape=[shape((rows, Q, D)), shape((rows, Q, D)), shape((4, r, D), F32), shape((r, FF), F32), shape((rd, D), F32),
                   shape((VROWS, 128), F32)],
        in_specs=[vm_spec, vm_spec] + [any_spec] * len(saved),
        out_specs=[any_spec, any_spec, vm_spec, vm_spec, vm_spec, vm_spec],
        scratch_shapes=[
            VMEM((4, D, D), BF), VMEM((D, FF), BF), VMEM((T, D), BF), VMEM((3, T, D), BF), VMEM((T, D), BF),
            VMEM((6, 8, T), F32), VMEM((T, D), BF), VMEM((T, D), F32), VMEM((T, 128), F32), VMEM((T, FF), BF),
            VMEM((T, FF), BF), VMEM((T, D), F32), VMEM((T, D), BF), VMEM((VROWS, D), F32), VMEM((VROWS, D), F32),
            VMEM((T, D), BF), VMEM((T, D), BF), VMEM((3, T, D), BF),
        ] + [VMEM((2, 2) + parts[i][:2], BF) for i in (0, 1, 3, 5, 6)]
        + bufs(lambda n, w, line: (2, 2, n, w)) + bufs(lambda n, w, line: (2, 2, n, w))
        + bufs(lambda n, w, line: (2, 2, n // 2, w)) + bufs(lambda n, w, line: (2, n // 2, w))
        + bufs(lambda n, w, line: (4, n // 4, w)) + bufs(lambda n, w, line: (5 if line else 3, n // 4, w)) + [
            VMEM((4, VROWS, D), F32), VMEM((6, VROWS, D), F32),
        ] + sems,
        compiler_params=pltpu.CompilerParams(collective_id=1, has_side_effects=True, vmem_limit_bytes=61 * 2**20),
    )
    reduced = bwd(segment_ids, pad_mask, *kept)

    def line_of(n):
        return shape((1, n), F32)

    done = pl.pallas_call(
        finish_kernel,
        name="finish",
        out_shape=[shape((rows, Q, D)), shape((rows, Q, D))] + [shape((r, D), F32)] * 4 + [shape((r, FF), F32), shape((rd, D), F32)]
        + [line_of(r)] * 5 + [line_of(4 * r)] + [line_of(r)] * 3,
        in_specs=[any_spec] * 5 + [vm_spec],
        out_specs=[any_spec] * 8 + [vm_spec] * 9,
        scratch_shapes=[VMEM((rows, Q, D), BF), VMEM((rows, Q, D), BF), VMEM((4, r, D), F32), VMEM((r, FF), F32), VMEM((rd, D), F32),
                        pltpu.SemaphoreType.DMA((13,))],
        compiler_params=pltpu.CompilerParams(vmem_limit_bytes=60 * 2**20),
    )(*reduced)
    block_out, grad_in, gq, gk, gvv, go, gu, gd = done[:8]
    bq, bv, bo, ga, sa, bu, bd, gf, sf = [v.reshape(-1) for v in done[8:]]
    grads = [gq, bq, gk, gvv, bv, go, bo, ga, sa, gu, bu, gd, bd, gf, sf]
    if fold > 1:
        def narrow(g):
            n = g.shape[0]
            whole = jnp.zeros((32 * n,) + g.shape[1:], F32)
            whole = lax.dynamic_update_slice_in_dim(whole, g, part * n, 0)
            return lax.psum_scatter(whole, ("batch", "seq"), scatter_dimension=0, tiled=True)
        grads = [narrow(g) for g in grads]
    return (block_out, grad_in) + tuple(grads)


def solution(mesh):
    fold = mesh.shape["batch"] // 8
    mat, vec = P(("batch", "seq"), None), P(("batch", "seq"))
    act, rows = P("batch", "seq", None), P("batch", None)
    kinds = [mat, vec, mat, mat, vec, mat, vec, vec, vec, mat, vec, mat, vec, vec, vec]
    return jax.shard_map(
        lambda *args: per_device(fold, *args),
        mesh=mesh,
        in_specs=tuple([act, rows, rows, act] + kinds),
        out_specs=tuple([act, act] + kinds),
        check_vma=False,
    )
```
